32 devices in a mesh: row: 8 (over y, x, core), col: 4 (over z).
Axes of the slice: x: 2, y: 2, z: 4, core: 2. Of those that a mesh axis runs over, the one named last changes fastest.
Arguments:
- features: bfloat16 [6144, 256], P(('row', 'col')), may hold values from -6 to 6
- weight: bfloat16 [256, 256], replicated, may hold values from -0.375 to 0.375
- tiles: bfloat16 [8, 4, 256, 64, 128], P('row', 'col'), may hold values from -0.0546875 to 0.0546875
- tile_rows: int32 [8, 4, 512], P('row', 'col'), may hold values from 0 to 11
- tile_cols: int32 [8, 4, 512], P('row', 'col'), may hold values from 0 to 23
- counts: int32 [8, 4], P('row', 'col'), may hold values from 128 to 512, as said below
Outputs:
- output: bfloat16 [6144, 256], P(('row', 'col'))
The draws below stay inside these ranges and needn't reach their ends.
Inputs may be any that keep to these rules, and one draw needn't show every extreme that they name: `counts`: some grid cell has exactly 512 live slots.
All inputs are finite; a program needn't handle non-finite values.
Results may differ from the reference program's by a relative error of at most 0.0049.
Values may be sent and summed in bfloat16 or wider, within the bound.
A program may use at most 64 MiB of HBM per device.

```python
import jax
import jax.numpy as jnp
from jax import lax

F = 256
TILE = 64
S = 192
TPD = 512
NODES = 6144
ROWT = 12
COLT = 24
N_ROW = 8
N_COL = 4


def draw_counts(key, part):
    first_key, second_key = jax.random.split(jax.random.fold_in(key, 17))
    values = jax.random.randint(first_key, (N_ROW * N_COL,), TPD // 4, TPD + 1, dtype=jnp.int32)
    location = jax.random.randint(second_key, (), 0, N_ROW * N_COL, dtype=jnp.int32)
    values = values.at[location].set(TPD)
    return values.reshape(N_ROW, N_COL)


def touch_ends(drawn, own_key, low, top_value):
    dims = drawn.shape
    spot = [jax.random.randint(jax.random.fold_in(own_key, axis), (), 0, dims[axis]) for axis in range(len(dims))]
    drawn = drawn.at[tuple(spot)].set(low)
    longest = dims.index(max(dims))
    spot[longest] = (spot[longest] + 1) % dims[longest]
    return drawn.at[tuple(spot)].set(top_value)


def shard_levels(rng, extent, shards, smallest, largest):
    level, own = 1.0, jax.random.fold_in(rng, 6)
    for position, shards_of in shards:
        steps = jnp.exp(jax.random.uniform(jax.random.fold_in(own, position), (shards_of,), jnp.float32, smallest / len(shards), largest / len(shards)))
        level = level * jnp.repeat(steps, extent[position] // shards_of).reshape([-1 if axis == position else 1 for axis in range(len(extent))])
    return level


def bell_draw(own_key, shape, deviation, bound, cuts=(), held_as=jnp.bfloat16):
    level = shard_levels(own_key, shape, cuts, -0.22, 0.18) if cuts else 1.0
    values = jax.random.normal(own_key, shape, jnp.float32) * deviation * level
    return jnp.minimum(jnp.maximum(values, -bound), bound).astype(held_as)


def setup_inputs(seed: int = 0) -> dict:
    streams_of = jax.random.split(jax.random.key(seed), 7)
    return {
        "features": bell_draw(streams_of[0], (NODES, F), 1.0, 6.0, ((0, 32),)),
        "weight": bell_draw(streams_of[1], (F, F), F ** -0.5, 0.375),
        "tiles": bell_draw(streams_of[2], (N_ROW, N_COL, TPD // 2, TILE, 2 * TILE), (TPD * TILE * TILE // S) ** -0.5, 0.0546875, ((0, 8), (1, 4))),
        "tile_rows": touch_ends(jax.random.randint(streams_of[3], (N_ROW, N_COL, TPD), 0, ROWT), jax.random.fold_in(streams_of[3], 1), 0, ROWT - 1).astype(jnp.int32),
        "tile_cols": touch_ends(jax.random.randint(streams_of[4], (N_ROW, N_COL, TPD), 0, COLT), jax.random.fold_in(streams_of[4], 1), 0, COLT - 1).astype(jnp.int32),
        "counts": draw_counts(jax.random.fold_in(streams_of[6], 71), 0),
    }


def reference(features, weight, tiles, tile_rows, tile_cols, counts):
    product = jnp.dot(features, weight, preferred_element_type=jnp.float32).astype(jnp.bfloat16)
    blocked = product.reshape(N_ROW, N_COL, S, F)
    row_tiles = N_COL * S // TILE
    col_tiles = N_ROW * S // TILE
    slot_index = jnp.arange(TPD, dtype=jnp.int32)

    def grid_row(carry, row_index):
        def add_column(total, col_index):
            column = lax.dynamic_index_in_dim(blocked, col_index, axis=1, keepdims=False)
            column = column.reshape(col_tiles, TILE, F)
            tile_pairs = tiles[row_index, col_index].astype(jnp.float32).reshape(TPD // 2, TILE, 2, TILE)
            picked = column[tile_cols[row_index, col_index]].astype(jnp.float32).reshape(TPD // 2, 2, TILE, F)
            terms = jnp.einsum('qajb,qjbf->qjaf', tile_pairs, picked).reshape(TPD, TILE, F)
            in_use = (slot_index < counts[row_index, col_index]).astype(jnp.float32)
            terms = terms * in_use[:, None, None]
            total = total + jax.ops.segment_sum(terms, tile_rows[row_index, col_index], num_segments=row_tiles)
            return total, None

        start = jnp.zeros((row_tiles, TILE, F), jnp.float32)
        total, unused = lax.scan(add_column, start, jnp.arange(N_COL, dtype=jnp.int32))
        result = jnp.maximum(total, 0.0).astype(jnp.bfloat16).reshape(row_tiles * TILE, F)
        return carry, result

    carry, rows_out = lax.scan(grid_row, jnp.zeros((), jnp.float32), jnp.arange(N_ROW, dtype=jnp.int32))
    return rows_out.reshape(N_ROW * N_COL * S, F)
```

```python
import functools

import jax
import jax.numpy as jnp
from jax import lax
from jax.experimental import pallas as pl
from jax.experimental.pallas import tpu as pltpu
from jax.sharding import PartitionSpec as P

TILE = 64
MESH = pl.DeviceIdType.MESH
CHUNKS = 8
GROUP = 4


def densify_kernel(counts_ref, rows_ref, cols_ref, tiles_ref, dense_ref, tile_buf, acc, sems):
    pairs = tiles_ref.shape[0]
    per_chunk = pairs // CHUNKS
    copies = []
    for k in range(CHUNKS):
        part = pl.ds(k * per_chunk, per_chunk)
        copy = pltpu.make_async_copy(tiles_ref.at[part], tile_buf.at[part], sems.at[k])
        copy.start()
        copies.append(copy)
    col_pairs = acc.shape[0]

    @pl.loop(0, col_pairs)
    def _(i):
        acc[i] = jnp.zeros(acc.shape[1:], acc.dtype)

    live = counts_ref[0]
    live_pairs = (live + 1) // 2
    lane_half = lax.broadcasted_iota(jnp.int32, (TILE, 2 * TILE), 1) // TILE
    low = lane_half == 0

    for k in range(CHUNKS):
        copies[k].wait()
        first = k * per_chunk
        groups = jnp.clip((live_pairs - first + GROUP - 1) // GROUP, 0, per_chunk // GROUP)

        @pl.loop(0, groups)
        def _(g):
            start = first + g * GROUP
            work = []
            for j in range(GROUP):
                q = start + j
                v = tile_buf[q].astype(jnp.float32)
                swapped = pltpu.roll(v, TILE, 1)
                work.append(jnp.where(low, v, swapped))
                work.append(jnp.where(low, swapped, v))
            for j in range(2 * GROUP):
                p = 2 * start + j
                r = rows_ref[p]
                c = cols_ref[p]
                half = jnp.where(p < live, c % 2, 2)
                at = (c // 2, pl.ds(pl.multiple_of(r * TILE, TILE), TILE))
                acc[at] += jnp.where(lane_half == half, work[j], 0.0)

    @pl.loop(0, col_pairs)
    def _(i):
        dense_ref[i] = acc[i].astype(dense_ref.dtype)


def densify(counts, rows, cols, tiles, row_tiles, col_tiles):
    shape = (col_tiles // 2, row_tiles * TILE, 2 * TILE)
    smem = pl.BlockSpec(memory_space=pltpu.SMEM)
    return pl.pallas_call(
        densify_kernel,
        out_shape=jax.ShapeDtypeStruct(shape, jnp.bfloat16),
        in_specs=[smem, smem, smem, pl.BlockSpec(memory_space=pl.ANY)],
        out_specs=pl.BlockSpec(memory_space=pltpu.VMEM),
        scratch_shapes=[
            pltpu.VMEM(tiles.shape, tiles.dtype),
            pltpu.VMEM(shape, jnp.float32),
            pltpu.SemaphoreType.DMA((CHUNKS,)),
        ],
        compiler_params=pltpu.CompilerParams(vmem_limit_bytes=24 << 20),
        cost_estimate=pl.CostEstimate(
            flops=20_000_000_000, bytes_accessed=2 * tiles.size, transcendentals=0
        ),
    )(counts, rows, cols, tiles)


def flip(index, mask, n):
    out, bit = 0, 1
    while bit < n:
        have = (index // bit) % 2
        out = out + bit * ((1 - have) if mask & bit else have)
        bit *= 2
    return out


def combine_kernel(n_row, n_col, *refs):
    pieces = refs[:n_row]
    (weight_ref, dense_ref, out_ref, table, send, recv, send_sems, recv_sems) = refs[n_row:]
    me_row, me = lax.axis_index("row"), lax.axis_index("col")
    block = out_ref.shape[0]
    barrier = pltpu.get_barrier_semaphore()
    for j in range(1, n_col):
        pl.semaphore_signal(
            barrier, inc=1, device_id=(me_row, (me + j) % n_col), device_id_type=MESH
        )
    weight = weight_ref[...]
    for s in range(n_row):
        at = pl.multiple_of(flip(me_row, s, n_row) * block, block)
        table[pl.ds(at, block)] = jnp.dot(
            pieces[s][...], weight, preferred_element_type=jnp.float32
        ).astype(table.dtype)
    product = table[...]

    def partial(owner):
        at = pl.ds(pl.multiple_of(owner * block, block), block)
        left = jnp.concatenate([dense_ref[i, at] for i in range(dense_ref.shape[0])], axis=1)
        return jnp.dot(left, product, preferred_element_type=jnp.float32)

    copies = []
    for j in range(1, n_col):
        peer = (me + j) % n_col
        send[j - 1] = partial(peer).astype(send.dtype)
        if j == 1:
            pl.semaphore_wait(barrier, n_col - 1)
        copy = pltpu.make_async_remote_copy(
            src_ref=send.at[j - 1],
            dst_ref=recv.at[j - 1],
            send_sem=send_sems.at[j - 1],
            recv_sem=recv_sems.at[j - 1],
            device_id=(me_row, peer),
            device_id_type=MESH,
        )
        copy.start()
        copies.append(copy)
    total = partial(me)
    for j in range(n_col - 1):
        copies[j].wait_recv()
        total = total + recv[j].astype(jnp.float32)
    out_ref[...] = jnp.maximum(total, 0.0).astype(out_ref.dtype)
    for copy in copies:
        copy.wait_send()


def fast_body(n_row, n_col, features, weight, tiles, tile_rows, tile_cols, counts):
    block, width = features.shape
    pieces = [features]
    for s in range(1, n_row):
        pieces.append(lax.ppermute(features, "row", [(i, i ^ s) for i in range(n_row)]))
    dense = densify(
        counts.reshape(1),
        tile_rows.reshape(-1),
        tile_cols.reshape(-1),
        tiles[0, 0],
        n_col * block // TILE,
        n_row * block // TILE,
    )
    vmem = pl.BlockSpec(memory_space=pltpu.VMEM)
    return pl.pallas_call(
        functools.partial(combine_kernel, n_row, n_col),
        out_shape=jax.ShapeDtypeStruct((block, width), jnp.bfloat16),
        in_specs=[vmem] * (n_row + 2),
        out_specs=vmem,
        scratch_shapes=[
            pltpu.VMEM((n_row * block, width), jnp.bfloat16),
            pltpu.VMEM((n_col - 1, block, width), jnp.bfloat16),
            pltpu.VMEM((n_col - 1, block, width), jnp.bfloat16),
            pltpu.SemaphoreType.DMA((n_col - 1,)),
            pltpu.SemaphoreType.DMA((n_col - 1,)),
        ],
        compiler_params=pltpu.CompilerParams(
            collective_id=0, has_side_effects=True, vmem_limit_bytes=24 << 20
        ),
    )(*pieces, weight, dense)


def general_body(features, weight, tiles, tile_rows, tile_cols, counts):
    feature_width = weight.shape[1]
    product_rows = jnp.dot(features, weight, preferred_element_type=jnp.float32).astype(
        jnp.bfloat16
    )
    gathered = lax.all_gather(product_rows, "row", axis=0, tiled=True)
    column_table = gathered.reshape(gathered.shape[0] // TILE, TILE, feature_width)
    row_tiles = lax.axis_size("col") * features.shape[0] // TILE
    slot_count = tile_rows.shape[2]
    block_size = min(64, slot_count)
    half_block = block_size // 2
    passes = slot_count // block_size
    pair_list = tiles[0, 0]
    row_list = tile_rows[0, 0]
    col_list = tile_cols[0, 0]
    live_count = counts[0, 0]
    block_slots = jnp.arange(block_size, dtype=jnp.int32)

    def add_block(block_index, total):
        first = block_index * block_size
        pair_block = lax.dynamic_slice_in_dim(pair_list, block_index * half_block, half_block, 0)
        pair_block = pair_block.reshape(half_block, TILE, 2, TILE)
        row_block = lax.dynamic_slice_in_dim(row_list, first, block_size, 0)
        col_block = lax.dynamic_slice_in_dim(col_list, first, block_size, 0)
        picked = column_table[col_block].reshape(half_block, 2, TILE, feature_width)
        terms = jnp.einsum(
            "qajb,qjbf->qjaf", pair_block, picked, preferred_element_type=jnp.float32
        )
        terms = terms.reshape(block_size, TILE, feature_width)
        in_use = (first + block_slots < live_count).astype(jnp.float32)
        terms = terms * in_use[:, None, None]
        return total.at[row_block].add(terms)

    zero_total = jnp.zeros((row_tiles, TILE, feature_width), jnp.float32)
    total = lax.fori_loop(0, passes, add_block, zero_total)
    partial_value = total.reshape(row_tiles * TILE, feature_width)
    own_rows = lax.psum_scatter(partial_value, "col", scatter_dimension=0, tiled=True)
    return jnp.maximum(own_rows, 0.0).astype(jnp.bfloat16)


def solution(mesh):
    n_row, n_col = mesh.shape["row"], mesh.shape["col"]
    power_of_two = n_row & (n_row - 1) == 0
    fast = power_of_two and n_row * n_col <= 64
    body = functools.partial(fast_body, n_row, n_col) if fast else general_body
    return jax.shard_map(
        body,
        mesh=mesh,
        in_specs=(
            P(("row", "col"), None),
            P(),
            P("row", "col", None, None, None),
            P("row", "col", None),
            P("row", "col", None),
            P("row", "col"),
        ),
        out_specs=P(("row", "col"), None),
        check_vma=False,
    )
```

```python
import functools

import jax
import jax.numpy as jnp
from jax import lax
from jax.experimental import pallas as pl
from jax.experimental.pallas import tpu as pltpu
from jax.sharding import PartitionSpec as P

TILE = 64
MESH = pl.DeviceIdType.MESH
CHUNKS = 8
GROUP = 4


def densify_kernel(
    counts_hbm, rows_hbm, cols_hbm, tiles_ref, dense_ref, counts, rows, cols, tile_buf, acc, rounded,
    sems, index_sems, out_sems,
):
    pairs = tiles_ref.shape[2]
    per_chunk = pairs // CHUNKS
    index_copies = []
    for k, (src, dst) in enumerate(((counts_hbm, counts), (rows_hbm, rows), (cols_hbm, cols))):
        copy = pltpu.make_async_copy(src, dst, index_sems.at[k])
        copy.start()
        index_copies.append(copy)
    copies = []
    for k in range(CHUNKS):
        part = pl.ds(k * per_chunk, per_chunk)
        copy = pltpu.make_async_copy(tiles_ref.at[0, 0, part], tile_buf.at[part], sems.at[k])
        copy.start()
        copies.append(copy)
    col_pairs = acc.shape[0]

    @pl.loop(0, col_pairs)
    def _(i):
        acc[i] = jnp.zeros(acc.shape[1:], acc.dtype)

    for copy in index_copies:
        copy.wait()
    live = counts[0, 0]
    live_pairs = (live + 1) // 2
    lane_half = lax.broadcasted_iota(jnp.int32, (TILE, 2 * TILE), 1) // TILE
    low = lane_half == 0

    for k in range(CHUNKS):
        copies[k].wait()
        first = k * per_chunk
        groups = jnp.clip((live_pairs - first + GROUP - 1) // GROUP, 0, per_chunk // GROUP)

        @pl.loop(0, groups)
        def _(g):
            start = first + g * GROUP
            work = []
            for j in range(GROUP):
                q = start + j
                v = tile_buf[q].astype(jnp.float32)
                swapped = pltpu.roll(v, TILE, 1)
                work.append(jnp.where(low, v, swapped))
                work.append(jnp.where(low, swapped, v))
            for j in range(2 * GROUP):
                p = 2 * start + j
                r = rows[0, 0, p]
                c = cols[0, 0, p]
                half = jnp.where(p < live, c % 2, 2)
                at = (c // 2, pl.ds(pl.multiple_of(r * TILE, TILE), TILE))
                acc[at] += jnp.where(lane_half == half, work[j], 0.0)

    out_copies = []
    for i in range(col_pairs):
        rounded[i] = acc[i].astype(rounded.dtype)
        copy = pltpu.make_async_copy(rounded.at[i], dense_ref.at[i], out_sems.at[i])
        copy.start()
        out_copies.append(copy)
    for copy in out_copies:
        copy.wait()


def densify(counts, rows, cols, tiles, row_tiles, col_tiles):
    shape = (col_tiles // 2, row_tiles * TILE, 2 * TILE)
    hbm = pl.BlockSpec(memory_space=pltpu.HBM)
    return pl.pallas_call(
        densify_kernel,
        out_shape=jax.ShapeDtypeStruct(shape, jnp.bfloat16),
        in_specs=[hbm] * 4,
        out_specs=hbm,
        scratch_shapes=[
            pltpu.SMEM(counts.shape, jnp.int32),
            pltpu.SMEM(rows.shape, jnp.int32),
            pltpu.SMEM(cols.shape, jnp.int32),
            pltpu.VMEM(tiles.shape[2:], tiles.dtype),
            pltpu.VMEM(shape, jnp.float32),
            pltpu.VMEM(shape, jnp.bfloat16),
            pltpu.SemaphoreType.DMA((CHUNKS,)),
            pltpu.SemaphoreType.DMA((3,)),
            pltpu.SemaphoreType.DMA((shape[0],)),
        ],
        compiler_params=pltpu.CompilerParams(vmem_limit_bytes=62 << 20),
        cost_estimate=pl.CostEstimate(
            flops=5_000_000_000, bytes_accessed=2 * tiles.size, transcendentals=0
        ),
    )(counts, rows, cols, tiles)


def flip(index, mask, n):
    out, bit = 0, 1
    while bit < n:
        have = (index // bit) % 2
        out = out + bit * ((1 - have) if mask & bit else have)
        bit *= 2
    return out


def combine_kernel(
    n_row, n_col, features_ref, weight_ref, dense_hbm, out_ref,
    dense_ref, dense_sem, table, send, recv, gather_send, gather_recv, send_sems, recv_sems,
):
    me_row, me = lax.axis_index("row"), lax.axis_index("col")
    block, width = out_ref.shape
    half_width = width // 2
    halves = range(2)
    dense_copy = pltpu.make_async_copy(dense_hbm, dense_ref, dense_sem.at[0])
    dense_copy.start()
    barrier = pltpu.get_barrier_semaphore()
    row_masks = [m for m in (1, 2, 4, 6) if m < n_row]
    far_masks = row_masks[1:]
    for m in row_masks:
        pl.semaphore_signal(
            barrier, inc=1, device_id=(flip(me_row, m, n_row), me), device_id_type=MESH
        )
    for j in range(1, n_col):
        pl.semaphore_signal(
            barrier, inc=1, device_id=(me_row, (me + j) % n_col), device_id_type=MESH
        )

    def rows_of(source):
        return pl.ds(pl.multiple_of(source * block, block), block)

    product = jnp.dot(features_ref[...], weight_ref[...], preferred_element_type=jnp.float32)
    product = product.astype(table.dtype)
    for h in halves:
        table[h, rows_of(me_row)] = product[:, h * half_width : (h + 1) * half_width]
    pl.semaphore_wait(barrier, len(row_masks) + n_col - 1)

    def gather_copy(h, piece, peer_mask):
        part = table.at[h, rows_of(flip(me_row, piece, n_row))]
        return pltpu.make_async_remote_copy(
            src_ref=part,
            dst_ref=part,
            send_sem=gather_send.at[h, piece ^ peer_mask],
            recv_sem=gather_recv.at[h, piece ^ peer_mask],
            device_id=(flip(me_row, peer_mask, n_row), me),
            device_id_type=MESH,
        )

    direct = [{m: gather_copy(h, 0, m) for m in row_masks} for h in halves]
    forward = [{m: gather_copy(h, m, 1) for m in far_masks} for h in halves]
    for h in halves:
        for m in reversed(row_masks):
            direct[h][m].start()

    def gather_half(h):
        for m in far_masks:
            direct[h][m].wait_recv()
            forward[h][m].start()
        direct[h][1].wait_recv()
        for m in far_masks:
            forward[h][m].wait_recv()

    def left_of(owner):
        at = rows_of(owner)
        return jnp.concatenate([dense_ref[i, at] for i in range(dense_ref.shape[0])], axis=1)

    def partial(h, owner):
        return jnp.dot(left_of(owner), table[h], preferred_element_type=jnp.float32)

    copies = []
    for h in halves:
        gather_half(h)
        if h == 0:
            dense_copy.wait()
        for j in (2, 1, 3):
            peer = (me + j) % n_col
            send[h, j - 1] = partial(h, peer).astype(send.dtype)
            copy = pltpu.make_async_remote_copy(
                src_ref=send.at[h, j - 1],
                dst_ref=recv.at[h, j - 1],
                send_sem=send_sems.at[h, j - 1],
                recv_sem=recv_sems.at[h, j - 1],
                device_id=(me_row, peer),
                device_id_type=MESH,
            )
            copy.start()
            copies.append((h, j, copy))
    totals = [partial(h, me) for h in halves]
    for h, j, copy in copies:
        copy.wait_recv()
        totals[h] = totals[h] + recv[h, j - 1].astype(jnp.float32)
    for h in halves:
        out_ref[:, h * half_width : (h + 1) * half_width] = jnp.maximum(totals[h], 0.0).astype(
            out_ref.dtype
        )
    for h in halves:
        for m in row_masks:
            direct[h][m].wait_send()
        for m in far_masks:
            forward[h][m].wait_send()
    for h, j, copy in copies:
        copy.wait_send()


def fast_body(n_row, n_col, features, weight, tiles, tile_rows, tile_cols, counts):
    block, width = features.shape
    dense = densify(
        counts, tile_rows, tile_cols, tiles, n_col * block // TILE, n_row * block // TILE
    )
    vmem = pl.BlockSpec(memory_space=pltpu.VMEM)
    return pl.pallas_call(
        functools.partial(combine_kernel, n_row, n_col),
        out_shape=jax.ShapeDtypeStruct((block, width), jnp.bfloat16),
        in_specs=[vmem, vmem, pl.BlockSpec(memory_space=pltpu.HBM)],
        out_specs=vmem,
        scratch_shapes=[
            pltpu.VMEM(dense.shape, dense.dtype),
            pltpu.SemaphoreType.DMA((1,)),
            pltpu.VMEM((2, n_row * block, width // 2), jnp.bfloat16),
            pltpu.VMEM((2, n_col - 1, block, width // 2), jnp.bfloat16),
            pltpu.VMEM((2, n_col - 1, block, width // 2), jnp.bfloat16),
            pltpu.SemaphoreType.DMA((2, n_row)),
            pltpu.SemaphoreType.DMA((2, n_row)),
            pltpu.SemaphoreType.DMA((2, n_col - 1)),
            pltpu.SemaphoreType.DMA((2, n_col - 1)),
        ],
        compiler_params=pltpu.CompilerParams(
            collective_id=0, has_side_effects=True, vmem_limit_bytes=62 << 20
        ),
    )(features, weight, dense)


def general_body(features, weight, tiles, tile_rows, tile_cols, counts):
    feature_width = weight.shape[1]
    product_rows = jnp.dot(features, weight, preferred_element_type=jnp.float32).astype(
        jnp.bfloat16
    )
    gathered = lax.all_gather(product_rows, "row", axis=0, tiled=True)
    column_table = gathered.reshape(gathered.shape[0] // TILE, TILE, feature_width)
    row_tiles = lax.axis_size("col") * features.shape[0] // TILE
    slot_count = tile_rows.shape[2]
    block_size = min(64, slot_count)
    half_block = block_size // 2
    passes = slot_count // block_size
    pair_list = tiles[0, 0]
    row_list = tile_rows[0, 0]
    col_list = tile_cols[0, 0]
    live_count = counts[0, 0]
    block_slots = jnp.arange(block_size, dtype=jnp.int32)

    def add_block(block_index, total):
        first = block_index * block_size
        pair_block = lax.dynamic_slice_in_dim(pair_list, block_index * half_block, half_block, 0)
        pair_block = pair_block.reshape(half_block, TILE, 2, TILE)
        row_block = lax.dynamic_slice_in_dim(row_list, first, block_size, 0)
        col_block = lax.dynamic_slice_in_dim(col_list, first, block_size, 0)
        picked = column_table[col_block].reshape(half_block, 2, TILE, feature_width)
        terms = jnp.einsum(
            "qajb,qjbf->qjaf", pair_block, picked, preferred_element_type=jnp.float32
        )
        terms = terms.reshape(block_size, TILE, feature_width)
        in_use = (first + block_slots < live_count).astype(jnp.float32)
        terms = terms * in_use[:, None, None]
        return total.at[row_block].add(terms)

    zero_total = jnp.zeros((row_tiles, TILE, feature_width), jnp.float32)
    total = lax.fori_loop(0, passes, add_block, zero_total)
    partial_value = total.reshape(row_tiles * TILE, feature_width)
    own_rows = lax.psum_scatter(partial_value, "col", scatter_dimension=0, tiled=True)
    return jnp.maximum(own_rows, 0.0).astype(jnp.bfloat16)


def solution(mesh):
    n_row, n_col = mesh.shape["row"], mesh.shape["col"]
    fast = (n_row, n_col) == (8, 4)
    body = functools.partial(fast_body, n_row, n_col) if fast else general_body
    return jax.shard_map(
        body,
        mesh=mesh,
        in_specs=(
            P(("row", "col"), None),
            P(),
            P("row", "col", None, None, None),
            P("row", "col", None),
            P("row", "col", None),
            P("row", "col"),
        ),
        out_specs=P(("row", "col"), None),
        check_vma=False,
    )
```

```python
import functools

import jax
import jax.numpy as jnp
from jax import lax
from jax.experimental import pallas as pl
from jax.experimental.pallas import tpu as pltpu
from jax.sharding import PartitionSpec as P

TILE = 64
MESH = pl.DeviceIdType.MESH
CHUNKS = 8
GROUP = 4


def densify_kernel(
    counts, rows_hbm, cols_hbm, tiles_ref, dense_ref, rows, cols, tile_buf, acc, rounded,
    sems, index_sems, out_sems,
):
    pairs = tiles_ref.shape[2]
    per_chunk = pairs // CHUNKS
    index_copies = []
    for k, (src, dst) in enumerate(((rows_hbm, rows), (cols_hbm, cols))):
        copy = pltpu.make_async_copy(src, dst, index_sems.at[k])
        copy.start()
        index_copies.append(copy)
    copies = []
    for k in range(CHUNKS):
        part = pl.ds(k * per_chunk, per_chunk)
        copy = pltpu.make_async_copy(tiles_ref.at[0, 0, part], tile_buf.at[part], sems.at[k])
        copy.start()
        copies.append(copy)
    col_pairs = acc.shape[0]

    @pl.loop(0, col_pairs)
    def _(i):
        acc[i] = jnp.zeros(acc.shape[1:], acc.dtype)

    for copy in index_copies:
        copy.wait()
    live = counts[0, 0]
    live_pairs = (live + 1) // 2
    lane_half = lax.broadcasted_iota(jnp.int32, (TILE, 2 * TILE), 1) // TILE
    low = lane_half == 0

    for k in range(CHUNKS):
        copies[k].wait()
        first = k * per_chunk
        groups = jnp.clip((live_pairs - first + GROUP - 1) // GROUP, 0, per_chunk // GROUP)

        @pl.loop(0, groups)
        def _(g):
            start = first + g * GROUP
            work = []
            for j in range(GROUP):
                q = start + j
                v = tile_buf[q].astype(jnp.float32)
                swapped = pltpu.roll(v, TILE, 1)
                work.append(jnp.where(low, v, swapped))
                work.append(jnp.where(low, swapped, v))
            for j in range(0, 2 * GROUP, 2):
                p = 2 * start + j
                r0, c0, r1, c1 = rows[0, 0, p], cols[0, 0, p], rows[0, 0, p + 1], cols[0, 0, p + 1]
                half0 = jnp.where(p < live, c0 % 2, 2)
                half1 = jnp.where(p + 1 < live, c1 % 2, 2)
                same = jnp.logical_and(r0 == r1, c0 // 2 == c1 // 2)
                at0 = (c0 // 2, pl.ds(pl.multiple_of(r0 * TILE, TILE), TILE))
                at1 = (c1 // 2, pl.ds(pl.multiple_of(r1 * TILE, TILE), TILE))
                term0 = jnp.where(lane_half == half0, work[j], 0.0)
                term1 = jnp.where(lane_half == half1, work[j + 1], 0.0)
                again = jnp.where(lane_half == jnp.where(same, half0, 2), work[j], 0.0)
                sum0 = acc[at0] + term0
                sum1 = acc[at1] + (term1 + again)
                acc[at0] = sum0
                acc[at1] = sum1

    out_copies = []
    for i in range(col_pairs):
        rounded[i] = acc[i].astype(rounded.dtype)
        copy = pltpu.make_async_copy(rounded.at[i], dense_ref.at[i], out_sems.at[i])
        copy.start()
        out_copies.append(copy)
    for copy in out_copies:
        copy.wait()


def densify(counts, rows, cols, tiles, row_tiles, col_tiles):
    shape = (col_tiles // 2, row_tiles * TILE, 2 * TILE)
    hbm = pl.BlockSpec(memory_space=pltpu.HBM)
    return pl.pallas_call(
        densify_kernel,
        out_shape=jax.ShapeDtypeStruct(shape, jnp.bfloat16),
        in_specs=[pl.BlockSpec(memory_space=pltpu.VMEM)] + [hbm] * 3,
        out_specs=hbm,
        scratch_shapes=[
            pltpu.SMEM(rows.shape, jnp.int32),
            pltpu.SMEM(cols.shape, jnp.int32),
            pltpu.VMEM(tiles.shape[2:], tiles.dtype),
            pltpu.VMEM(shape, jnp.float32),
            pltpu.VMEM(shape, jnp.bfloat16),
            pltpu.SemaphoreType.DMA((CHUNKS,)),
            pltpu.SemaphoreType.DMA((2,)),
            pltpu.SemaphoreType.DMA((shape[0],)),
        ],
        compiler_params=pltpu.CompilerParams(vmem_limit_bytes=61 << 20),
        cost_estimate=pl.CostEstimate(
            flops=5_000_000_000, bytes_accessed=2 * tiles.size, transcendentals=0
        ),
    )(counts, rows, cols, tiles)


def flip(index, mask, n):
    out, bit = 0, 1
    while bit < n:
        have = (index // bit) % 2
        out = out + bit * ((1 - have) if mask & bit else have)
        bit *= 2
    return out


def combine_kernel(
    n_row, n_col, features_ref, weight_ref, dense_hbm, out_ref,
    dense_ref, dense_sem, table, send, recv, gather_send, gather_recv, send_sems, recv_sems,
):
    me_row, me = lax.axis_index("row"), lax.axis_index("col")
    block, width = out_ref.shape
    half_width = width // 2
    halves = range(2)
    dense_copy = pltpu.make_async_copy(dense_hbm, dense_ref, dense_sem.at[0])
    dense_copy.start()
    barrier = pltpu.get_barrier_semaphore()
    row_masks = [m for m in (1, 2, 4, 6) if m < n_row]
    far_masks = row_masks[1:]
    for m in row_masks:
        pl.semaphore_signal(
            barrier, inc=1, device_id=(flip(me_row, m, n_row), me), device_id_type=MESH
        )
    for j in range(1, n_col):
        pl.semaphore_signal(
            barrier, inc=1, device_id=(me_row, (me + j) % n_col), device_id_type=MESH
        )

    def rows_of(source):
        return pl.ds(pl.multiple_of(source * block, block), block)

    product = jnp.dot(features_ref[...], weight_ref[...], preferred_element_type=jnp.float32)
    product = product.astype(table.dtype)
    for h in halves:
        table[h, rows_of(me_row)] = product[:, h * half_width : (h + 1) * half_width]
    pl.semaphore_wait(barrier, len(row_masks) + n_col - 1)

    def gather_copy(h, piece, peer_mask):
        part = table.at[h, rows_of(flip(me_row, piece, n_row))]
        return pltpu.make_async_remote_copy(
            src_ref=part,
            dst_ref=part,
            send_sem=gather_send.at[h, piece ^ peer_mask],
            recv_sem=gather_recv.at[h, piece ^ peer_mask],
            device_id=(flip(me_row, peer_mask, n_row), me),
            device_id_type=MESH,
        )

    direct = [{m: gather_copy(h, 0, m) for m in row_masks} for h in halves]
    forward = [{m: gather_copy(h, m, 1) for m in far_masks} for h in halves]

    def start_half(h):
        for m in reversed(row_masks):
            direct[h][m].start()

    def finish_half(h):
        for m in far_masks:
            direct[h][m].wait_recv()
            forward[h][m].start()
        direct[h][1].wait_recv()
        for m in far_masks:
            forward[h][m].wait_recv()

    def left_of(owner):
        at = rows_of(owner)
        return jnp.concatenate([dense_ref[i, at] for i in range(dense_ref.shape[0])], axis=1)

    def partial(h, owner):
        return jnp.dot(left_of(owner), table[h], preferred_element_type=jnp.float32)

    copies = []
    start_half(0)
    for h in halves:
        finish_half(h)
        if h == 0:
            start_half(1)
            dense_copy.wait()
        for j in (2, 1, 3):
            peer = (me + j) % n_col
            send[h, j - 1] = partial(h, peer).astype(send.dtype)
            copy = pltpu.make_async_remote_copy(
                src_ref=send.at[h, j - 1],
                dst_ref=recv.at[h, j - 1],
                send_sem=send_sems.at[h, j - 1],
                recv_sem=recv_sems.at[h, j - 1],
                device_id=(me_row, peer),
                device_id_type=MESH,
            )
            copy.start()
            copies.append((h, j, copy))
    totals = [partial(h, me) for h in halves]
    for h, j, copy in copies:
        copy.wait_recv()
        totals[h] = totals[h] + recv[h, j - 1].astype(jnp.float32)
    for h in halves:
        out_ref[:, h * half_width : (h + 1) * half_width] = jnp.maximum(totals[h], 0.0).astype(
            out_ref.dtype
        )
    for h in halves:
        for m in row_masks:
            direct[h][m].wait_send()
        for m in far_masks:
            forward[h][m].wait_send()
    for h, j, copy in copies:
        copy.wait_send()


def fast_body(n_row, n_col, features, weight, tiles, tile_rows, tile_cols, counts):
    block, width = features.shape
    dense = densify(
        counts, tile_rows, tile_cols, tiles, n_col * block // TILE, n_row * block // TILE
    )
    vmem = pl.BlockSpec(memory_space=pltpu.VMEM)
    return pl.pallas_call(
        functools.partial(combine_kernel, n_row, n_col),
        out_shape=jax.ShapeDtypeStruct((block, width), jnp.bfloat16),
        in_specs=[vmem, vmem, pl.BlockSpec(memory_space=pltpu.HBM)],
        out_specs=vmem,
        scratch_shapes=[
            pltpu.VMEM(dense.shape, dense.dtype),
            pltpu.SemaphoreType.DMA((1,)),
            pltpu.VMEM((2, n_row * block, width // 2), jnp.bfloat16),
            pltpu.VMEM((2, n_col - 1, block, width // 2), jnp.bfloat16),
            pltpu.VMEM((2, n_col - 1, block, width // 2), jnp.bfloat16),
            pltpu.SemaphoreType.DMA((2, n_row)),
            pltpu.SemaphoreType.DMA((2, n_row)),
            pltpu.SemaphoreType.DMA((2, n_col - 1)),
            pltpu.SemaphoreType.DMA((2, n_col - 1)),
        ],
        compiler_params=pltpu.CompilerParams(
            collective_id=0, has_side_effects=True, vmem_limit_bytes=61 << 20
        ),
    )(features, weight, dense)


def general_body(features, weight, tiles, tile_rows, tile_cols, counts):
    feature_width = weight.shape[1]
    product_rows = jnp.dot(features, weight, preferred_element_type=jnp.float32).astype(
        jnp.bfloat16
    )
    gathered = lax.all_gather(product_rows, "row", axis=0, tiled=True)
    column_table = gathered.reshape(gathered.shape[0] // TILE, TILE, feature_width)
    row_tiles = lax.axis_size("col") * features.shape[0] // TILE
    slot_count = tile_rows.shape[2]
    block_size = min(64, slot_count)
    half_block = block_size // 2
    passes = slot_count // block_size
    pair_list = tiles[0, 0]
    row_list = tile_rows[0, 0]
    col_list = tile_cols[0, 0]
    live_count = counts[0, 0]
    block_slots = jnp.arange(block_size, dtype=jnp.int32)

    def add_block(block_index, total):
        first = block_index * block_size
        pair_block = lax.dynamic_slice_in_dim(pair_list, block_index * half_block, half_block, 0)
        pair_block = pair_block.reshape(half_block, TILE, 2, TILE)
        row_block = lax.dynamic_slice_in_dim(row_list, first, block_size, 0)
        col_block = lax.dynamic_slice_in_dim(col_list, first, block_size, 0)
        picked = column_table[col_block].reshape(half_block, 2, TILE, feature_width)
        terms = jnp.einsum(
            "qajb,qjbf->qjaf", pair_block, picked, preferred_element_type=jnp.float32
        )
        terms = terms.reshape(block_size, TILE, feature_width)
        in_use = (first + block_slots < live_count).astype(jnp.float32)
        terms = terms * in_use[:, None, None]
        return total.at[row_block].add(terms)

    zero_total = jnp.zeros((row_tiles, TILE, feature_width), jnp.float32)
    total = lax.fori_loop(0, passes, add_block, zero_total)
    partial_value = total.reshape(row_tiles * TILE, feature_width)
    own_rows = lax.psum_scatter(partial_value, "col", scatter_dimension=0, tiled=True)
    return jnp.maximum(own_rows, 0.0).astype(jnp.bfloat16)


def solution(mesh):
    n_row, n_col = mesh.shape["row"], mesh.shape["col"]
    fast = (n_row, n_col) == (8, 4)
    body = functools.partial(fast_body, n_row, n_col) if fast else general_body
    return jax.shard_map(
        body,
        mesh=mesh,
        in_specs=(
            P(("row", "col"), None),
            P(),
            P("row", "col", None, None, None),
            P("row", "col", None),
            P("row", "col", None),
            P("row", "col"),
        ),
        out_specs=P(("row", "col"), None),
        check_vma=False,
    )
```

```python
import functools

import jax
import jax.numpy as jnp
from jax import lax
from jax.experimental import pallas as pl
from jax.experimental.pallas import tpu as pltpu
from jax.sharding import PartitionSpec as P

TILE = 64
MESH = pl.DeviceIdType.MESH
CHUNKS = 8
GROUP = 8


def densify_kernel(
    counts, rows_hbm, cols_hbm, tiles_ref, dense_ref, rows, cols, tile_buf, acc, rounded, masks,
    sems, index_sems, out_sems,
):
    pairs = tiles_ref.shape[2]
    per_chunk = pairs // CHUNKS
    index_copies = []
    for k, (src, dst) in enumerate(((rows_hbm, rows), (cols_hbm, cols))):
        copy = pltpu.make_async_copy(src, dst, index_sems.at[k])
        copy.start()
        index_copies.append(copy)
    copies = []
    for k in range(CHUNKS):
        part = pl.ds(k * per_chunk, per_chunk)
        copy = pltpu.make_async_copy(tiles_ref.at[0, 0, part], tile_buf.at[part], sems.at[k])
        copy.start()
        copies.append(copy)
    col_pairs = acc.shape[0]

    @pl.loop(0, col_pairs)
    def _(i):
        acc[i] = jnp.zeros(acc.shape[1:], acc.dtype)

    for copy in index_copies:
        copy.wait()
    live = counts[0, 0]
    live_pairs = (live + 1) // 2
    lane_half = lax.broadcasted_iota(jnp.int32, masks.shape[1:], 1) // TILE
    for half in range(2):
        masks[half] = (lane_half == half).astype(masks.dtype)
    masks[2] = jnp.zeros(masks.shape[1:], masks.dtype)
    source = lax.broadcasted_iota(jnp.int32, (2 * TILE, 4 * TILE), 0)
    target = lax.broadcasted_iota(jnp.int32, (2 * TILE, 4 * TILE), 1)
    spread = (source == target // (2 * TILE) * TILE + target % TILE).astype(jnp.float32)
    spread = spread.astype(jnp.bfloat16)
    octets = TILE // 8

    for k in range(CHUNKS):
        copies[k].wait()
        first = k * per_chunk
        groups = jnp.clip((live_pairs - first + GROUP - 1) // GROUP, 0, per_chunk // GROUP)

        @pl.loop(0, groups)
        def _(g):
            start = first + g * GROUP
            both = tile_buf[pl.ds(start, GROUP)].reshape(GROUP * TILE, 2 * TILE)
            both = jnp.dot(both, spread, preferred_element_type=jnp.float32)
            for j in range(GROUP):
                p = 2 * (start + j)
                mine = slice(j * TILE, (j + 1) * TILE)
                tile0 = both[mine, : 2 * TILE].reshape(octets, 8, 2 * TILE)
                tile1 = both[mine, 2 * TILE :].reshape(octets, 8, 2 * TILE)
                r0, c0, r1, c1 = rows[0, 0, p], cols[0, 0, p], rows[0, 0, p + 1], cols[0, 0, p + 1]
                half0 = jnp.where(p < live, c0 % 2, 2)
                half1 = jnp.where(p + 1 < live, c1 % 2, 2)
                same = jnp.logical_and(r0 == r1, c0 // 2 == c1 // 2)
                at0 = (c0 // 2, pl.ds(r0 * octets, octets))
                at1 = (c1 // 2, pl.ds(r1 * octets, octets))
                term0 = tile0 * masks[half0][None]
                term1 = tile1 * masks[half1][None]
                again = tile0 * masks[jnp.where(same, half0, 2)][None]
                sum0 = acc[at0] + term0
                sum1 = acc[at1] + (term1 + again)
                acc[at0] = sum0
                acc[at1] = sum1

    out_copies = []
    for i in range(col_pairs):
        rounded[i] = acc[i].reshape(rounded.shape[1:]).astype(rounded.dtype)
        copy = pltpu.make_async_copy(rounded.at[i], dense_ref.at[i], out_sems.at[i])
        copy.start()
        out_copies.append(copy)
    for copy in out_copies:
        copy.wait()


def densify(counts, rows, cols, tiles, row_tiles, col_tiles):
    shape = (col_tiles // 2, row_tiles * TILE, 2 * TILE)
    hbm = pl.BlockSpec(memory_space=pltpu.HBM)
    return pl.pallas_call(
        densify_kernel,
        out_shape=jax.ShapeDtypeStruct(shape, jnp.bfloat16),
        in_specs=[pl.BlockSpec(memory_space=pltpu.VMEM)] + [hbm] * 3,
        out_specs=hbm,
        scratch_shapes=[
            pltpu.SMEM(rows.shape, jnp.int32),
            pltpu.SMEM(cols.shape, jnp.int32),
            pltpu.VMEM(tiles.shape[2:], tiles.dtype),
            pltpu.VMEM((shape[0], shape[1] // 8, 8, shape[2]), jnp.float32),
            pltpu.VMEM(shape, jnp.bfloat16),
            pltpu.VMEM((3, 8, 2 * TILE), jnp.float32),
            pltpu.SemaphoreType.DMA((CHUNKS,)),
            pltpu.SemaphoreType.DMA((2,)),
            pltpu.SemaphoreType.DMA((shape[0],)),
        ],
        compiler_params=pltpu.CompilerParams(vmem_limit_bytes=61 << 20),
        cost_estimate=pl.CostEstimate(
            flops=5_000_000_000, bytes_accessed=2 * tiles.size, transcendentals=0
        ),
    )(counts, rows, cols, tiles)


def flip(index, mask, n):
    out, bit = 0, 1
    while bit < n:
        have = (index // bit) % 2
        out = out + bit * ((1 - have) if mask & bit else have)
        bit *= 2
    return out


def combine_kernel(
    n_row, n_col, features_ref, weight_ref, dense_hbm, out_ref,
    dense_ref, dense_sem, table, send, recv, gather_send, gather_recv, send_sems, recv_sems,
):
    me_row, me = lax.axis_index("row"), lax.axis_index("col")
    block = out_ref.shape[0]
    barrier = pltpu.get_barrier_semaphore()
    for m in range(1, n_row):
        pl.semaphore_signal(
            barrier, inc=1, device_id=(flip(me_row, m, n_row), me), device_id_type=MESH
        )
    for j in range(1, n_col):
        pl.semaphore_signal(
            barrier, inc=1, device_id=(me_row, (me + j) % n_col), device_id_type=MESH
        )
    dense_copy = pltpu.make_async_copy(dense_hbm, dense_ref, dense_sem.at[0])
    dense_copy.start()

    def rows_of(source):
        return pl.ds(pl.multiple_of(source * block, block), block)

    product = jnp.dot(features_ref[...], weight_ref[...], preferred_element_type=jnp.float32)
    table[rows_of(me_row)] = product.astype(table.dtype)
    pl.semaphore_wait(barrier, n_row - 1 + n_col - 1)

    pieces = []
    for m in reversed(range(1, n_row)):
        part = table.at[rows_of(me_row)]
        copy = pltpu.make_async_remote_copy(
            src_ref=part,
            dst_ref=part,
            send_sem=gather_send.at[m],
            recv_sem=gather_recv.at[m],
            device_id=(flip(me_row, m, n_row), me),
            device_id_type=MESH,
        )
        copy.start()
        pieces.append(copy)
    dense_copy.wait()
    for copy in pieces:
        copy.wait_recv()

    def partial(owner):
        at = rows_of(owner)
        left = jnp.concatenate([dense_ref[i, at] for i in range(dense_ref.shape[0])], axis=1)
        return jnp.dot(left, table[...], preferred_element_type=jnp.float32)

    copies = []
    for j in (2, 1, 3):
        peer = (me + j) % n_col
        send[j - 1] = partial(peer).astype(send.dtype)
        copy = pltpu.make_async_remote_copy(
            src_ref=send.at[j - 1],
            dst_ref=recv.at[j - 1],
            send_sem=send_sems.at[j - 1],
            recv_sem=recv_sems.at[j - 1],
            device_id=(me_row, peer),
            device_id_type=MESH,
        )
        copy.start()
        copies.append((j, copy))
    total = partial(me)
    for j, copy in copies:
        copy.wait_recv()
        total = total + recv[j - 1].astype(jnp.float32)
    out_ref[...] = jnp.maximum(total, 0.0).astype(out_ref.dtype)
    for copy in pieces:
        copy.wait_send()
    for j, copy in copies:
        copy.wait_send()


def fast_body(n_row, n_col, features, weight, tiles, tile_rows, tile_cols, counts):
    block, width = features.shape
    dense = densify(
        counts, tile_rows, tile_cols, tiles, n_col * block // TILE, n_row * block // TILE
    )
    vmem = pl.BlockSpec(memory_space=pltpu.VMEM)
    return pl.pallas_call(
        functools.partial(combine_kernel, n_row, n_col),
        out_shape=jax.ShapeDtypeStruct((block, width), jnp.bfloat16),
        in_specs=[vmem, vmem, pl.BlockSpec(memory_space=pltpu.HBM)],
        out_specs=vmem,
        scratch_shapes=[
            pltpu.VMEM(dense.shape, dense.dtype),
            pltpu.SemaphoreType.DMA((1,)),
            pltpu.VMEM((n_row * block, width), jnp.bfloat16),
            pltpu.VMEM((n_col - 1, block, width), jnp.bfloat16),
            pltpu.VMEM((n_col - 1, block, width), jnp.bfloat16),
            pltpu.SemaphoreType.DMA((n_row,)),
            pltpu.SemaphoreType.DMA((n_row,)),
            pltpu.SemaphoreType.DMA((n_col - 1,)),
            pltpu.SemaphoreType.DMA((n_col - 1,)),
        ],
        compiler_params=pltpu.CompilerParams(
            collective_id=0, has_side_effects=True, vmem_limit_bytes=52 << 20
        ),
    )(features, weight, dense)


def general_body(features, weight, tiles, tile_rows, tile_cols, counts):
    feature_width = weight.shape[1]
    product_rows = jnp.dot(features, weight, preferred_element_type=jnp.float32).astype(
        jnp.bfloat16
    )
    gathered = lax.all_gather(product_rows, "row", axis=0, tiled=True)
    column_table = gathered.reshape(gathered.shape[0] // TILE, TILE, feature_width)
    row_tiles = lax.axis_size("col") * features.shape[0] // TILE
    slot_count = tile_rows.shape[2]
    block_size = min(64, slot_count)
    half_block = block_size // 2
    passes = slot_count // block_size
    pair_list = tiles[0, 0]
    row_list = tile_rows[0, 0]
    col_list = tile_cols[0, 0]
    live_count = counts[0, 0]
    block_slots = jnp.arange(block_size, dtype=jnp.int32)

    def add_block(block_index, total):
        first = block_index * block_size
        pair_block = lax.dynamic_slice_in_dim(pair_list, block_index * half_block, half_block, 0)
        pair_block = pair_block.reshape(half_block, TILE, 2, TILE)
        row_block = lax.dynamic_slice_in_dim(row_list, first, block_size, 0)
        col_block = lax.dynamic_slice_in_dim(col_list, first, block_size, 0)
        picked = column_table[col_block].reshape(half_block, 2, TILE, feature_width)
        terms = jnp.einsum(
            "qajb,qjbf->qjaf", pair_block, picked, preferred_element_type=jnp.float32
        )
        terms = terms.reshape(block_size, TILE, feature_width)
        in_use = (first + block_slots < live_count).astype(jnp.float32)
        terms = terms * in_use[:, None, None]
        return total.at[row_block].add(terms)

    zero_total = jnp.zeros((row_tiles, TILE, feature_width), jnp.float32)
    total = lax.fori_loop(0, passes, add_block, zero_total)
    partial_value = total.reshape(row_tiles * TILE, feature_width)
    own_rows = lax.psum_scatter(partial_value, "col", scatter_dimension=0, tiled=True)
    return jnp.maximum(own_rows, 0.0).astype(jnp.bfloat16)


def solution(mesh):
    n_row, n_col = mesh.shape["row"], mesh.shape["col"]
    fast = (n_row, n_col) == (8, 4)
    body = functools.partial(fast_body, n_row, n_col) if fast else general_body
    return jax.shard_map(
        body,
        mesh=mesh,
        in_specs=(
            P(("row", "col"), None),
            P(),
            P("row", "col", None, None, None),
            P("row", "col", None),
            P("row", "col", None),
            P("row", "col"),
        ),
        out_specs=P(("row", "col"), None),
        check_vma=False,
    )
```

```python
import functools

import jax
import jax.numpy as jnp
from jax import lax
from jax.experimental import pallas as pl
from jax.experimental.pallas import tpu as pltpu
from jax.sharding import PartitionSpec as P

TILE = 64
MESH = pl.DeviceIdType.MESH
CHUNKS = 8
GROUP = 8


def densify_kernel(
    counts, rows_hbm, cols_hbm, tiles_ref, dense_ref, rows, cols, tile_buf, acc, rounded, masks,
    sems, index_sems, out_sems,
):
    pairs = tiles_ref.shape[2]
    per_chunk = pairs // CHUNKS
    index_copies = []
    for k, (src, dst) in enumerate(((rows_hbm, rows), (cols_hbm, cols))):
        copy = pltpu.make_async_copy(src, dst, index_sems.at[k])
        copy.start()
        index_copies.append(copy)
    copies = []
    for k in range(CHUNKS):
        part = pl.ds(k * per_chunk, per_chunk)
        copy = pltpu.make_async_copy(tiles_ref.at[0, 0, part], tile_buf.at[part], sems.at[k])
        copy.start()
        copies.append(copy)
    col_pairs = rounded.shape[0]
    octets_per_pair = acc.shape[0] // col_pairs

    @pl.loop(0, col_pairs)
    def _(i):
        zeros = jnp.zeros((octets_per_pair, *acc.shape[1:]), acc.dtype)
        acc[pl.ds(i * octets_per_pair, octets_per_pair)] = zeros

    for copy in index_copies:
        copy.wait()
    live = counts[0, 0]
    live_pairs = (live + 1) // 2
    lane_half = lax.broadcasted_iota(jnp.int32, masks.shape[1:], 1) // TILE
    for half in range(2):
        masks[half] = (lane_half == half).astype(masks.dtype)
    masks[2] = jnp.zeros(masks.shape[1:], masks.dtype)
    source = lax.broadcasted_iota(jnp.int32, (2 * TILE, 4 * TILE), 0)
    target = lax.broadcasted_iota(jnp.int32, (2 * TILE, 4 * TILE), 1)
    spread = (source == target // (2 * TILE) * TILE + target % TILE).astype(jnp.float32)
    spread = spread.astype(jnp.bfloat16)
    octets = TILE // 8

    for k in range(CHUNKS):
        copies[k].wait()
        first = k * per_chunk
        groups = jnp.clip((live_pairs - first + GROUP - 1) // GROUP, 0, per_chunk // GROUP)

        @pl.loop(0, groups)
        def _(g):
            start = first + g * GROUP
            both = tile_buf[pl.ds(start, GROUP)].reshape(GROUP * TILE, 2 * TILE)
            both = jnp.dot(both, spread, preferred_element_type=jnp.float32)
            for j in range(GROUP):
                p = 2 * (start + j)
                mine = slice(j * TILE, (j + 1) * TILE)
                tile0 = both[mine, : 2 * TILE].reshape(octets, 8, 2 * TILE)
                tile1 = both[mine, 2 * TILE :].reshape(octets, 8, 2 * TILE)
                r0, c0, r1, c1 = rows[0, 0, p], cols[0, 0, p], rows[0, 0, p + 1], cols[0, 0, p + 1]
                half0 = jnp.where(p < live, c0 & 1, 2)
                half1 = jnp.where(p + 1 < live, c1 & 1, 2)
                place0 = lax.shift_right_logical(c0, 1) * octets_per_pair + r0 * octets
                place1 = lax.shift_right_logical(c1, 1) * octets_per_pair + r1 * octets
                same = place0 == place1
                at0 = pl.ds(place0, octets)
                at1 = pl.ds(place1, octets)
                term0 = tile0 * masks[half0][None]
                term1 = tile1 * masks[half1][None]
                again = tile0 * masks[jnp.where(same, half0, 2)][None]
                sum0 = acc[at0] + term0
                sum1 = acc[at1] + (term1 + again)
                acc[at0] = sum0
                acc[at1] = sum1

    out_copies = []
    for i in range(col_pairs):
        part = acc[i * octets_per_pair : (i + 1) * octets_per_pair]
        rounded[i] = part.reshape(rounded.shape[1:]).astype(rounded.dtype)
        copy = pltpu.make_async_copy(rounded.at[i], dense_ref.at[i], out_sems.at[i])
        copy.start()
        out_copies.append(copy)
    for copy in out_copies:
        copy.wait()


def densify(counts, rows, cols, tiles, row_tiles, col_tiles):
    shape = (col_tiles // 2, row_tiles * TILE, 2 * TILE)
    hbm = pl.BlockSpec(memory_space=pltpu.HBM)
    return pl.pallas_call(
        densify_kernel,
        out_shape=jax.ShapeDtypeStruct(shape, jnp.bfloat16),
        in_specs=[pl.BlockSpec(memory_space=pltpu.VMEM)] + [hbm] * 3,
        out_specs=hbm,
        scratch_shapes=[
            pltpu.SMEM(rows.shape, jnp.int32),
            pltpu.SMEM(cols.shape, jnp.int32),
            pltpu.VMEM(tiles.shape[2:], tiles.dtype),
            pltpu.VMEM((shape[0] * shape[1] // 8, 8, shape[2]), jnp.float32),
            pltpu.VMEM(shape, jnp.bfloat16),
            pltpu.VMEM((3, 8, 2 * TILE), jnp.float32),
            pltpu.SemaphoreType.DMA((CHUNKS,)),
            pltpu.SemaphoreType.DMA((2,)),
            pltpu.SemaphoreType.DMA((shape[0],)),
        ],
        compiler_params=pltpu.CompilerParams(vmem_limit_bytes=61 << 20),
        cost_estimate=pl.CostEstimate(
            flops=5_000_000_000, bytes_accessed=2 * tiles.size, transcendentals=0
        ),
    )(counts, rows, cols, tiles)


def flip(index, mask, n):
    out, bit = 0, 1
    while bit < n:
        have = (index // bit) % 2
        out = out + bit * ((1 - have) if mask & bit else have)
        bit *= 2
    return out


def combine_kernel(
    n_row, n_col, own_ref, x_ref, y_ref, across_ref, weight_ref, dense_hbm, out_ref,
    dense_ref, dense_sem, table, send, recv, gather_send, gather_recv, send_sems, recv_sems,
):
    me_row, me = lax.axis_index("row"), lax.axis_index("col")
    block = out_ref.shape[0]
    barrier = pltpu.get_barrier_semaphore()
    buddy = flip(me_row, 1, n_row)
    pl.semaphore_signal(barrier, inc=1, device_id=(buddy, me), device_id_type=MESH)
    for j in range(1, n_col):
        pl.semaphore_signal(
            barrier, inc=1, device_id=(me_row, (me + j) % n_col), device_id_type=MESH
        )
    dense_copy = pltpu.make_async_copy(dense_hbm, dense_ref, dense_sem.at[0])
    dense_copy.start()

    def rows_of(source):
        return pl.ds(pl.multiple_of(source * block, block), block)

    weight = weight_ref[...]
    sources = [flip(me_row, m, n_row) for m in (0, 2, 4, 6)]
    for source, ref in zip(sources, (own_ref, x_ref, y_ref, across_ref)):
        product = jnp.dot(ref[...], weight, preferred_element_type=jnp.float32)
        table[rows_of(source)] = product.astype(table.dtype)
    pl.semaphore_wait(barrier, n_col)

    pieces = []
    for k, source in enumerate(sources):
        part = table.at[rows_of(source)]
        copy = pltpu.make_async_remote_copy(
            src_ref=part,
            dst_ref=part,
            send_sem=gather_send.at[k],
            recv_sem=gather_recv.at[k],
            device_id=(buddy, me),
            device_id_type=MESH,
        )
        copy.start()
        pieces.append(copy)
    dense_copy.wait()
    for copy in pieces:
        copy.wait_recv()

    def partial(owner):
        at = rows_of(owner)
        left = jnp.concatenate([dense_ref[i, at] for i in range(dense_ref.shape[0])], axis=1)
        return jnp.dot(left, table[...], preferred_element_type=jnp.float32)

    copies = []
    for j in (2, 1, 3):
        peer = (me + j) % n_col
        send[j - 1] = partial(peer).astype(send.dtype)
        copy = pltpu.make_async_remote_copy(
            src_ref=send.at[j - 1],
            dst_ref=recv.at[j - 1],
            send_sem=send_sems.at[j - 1],
            recv_sem=recv_sems.at[j - 1],
            device_id=(me_row, peer),
            device_id_type=MESH,
        )
        copy.start()
        copies.append((j, copy))
    total = partial(me)
    for j, copy in copies:
        copy.wait_recv()
        total = total + recv[j - 1].astype(jnp.float32)
    out_ref[...] = jnp.maximum(total, 0.0).astype(out_ref.dtype)
    for copy in pieces:
        copy.wait_send()
    for j, copy in copies:
        copy.wait_send()


def fast_body(n_row, n_col, features, weight, tiles, tile_rows, tile_cols, counts):
    block, width = features.shape
    pieces = [features]
    for m in (2, 4, 6):
        pieces.append(lax.ppermute(features, "row", [(i, i ^ m) for i in range(n_row)]))
    dense = densify(
        counts, tile_rows, tile_cols, tiles, n_col * block // TILE, n_row * block // TILE
    )
    vmem = pl.BlockSpec(memory_space=pltpu.VMEM)
    return pl.pallas_call(
        functools.partial(combine_kernel, n_row, n_col),
        out_shape=jax.ShapeDtypeStruct((block, width), jnp.bfloat16),
        in_specs=[vmem] * 5 + [pl.BlockSpec(memory_space=pltpu.HBM)],
        out_specs=vmem,
        scratch_shapes=[
            pltpu.VMEM(dense.shape, dense.dtype),
            pltpu.SemaphoreType.DMA((1,)),
            pltpu.VMEM((n_row * block, width), jnp.bfloat16),
            pltpu.VMEM((n_col - 1, block, width), jnp.bfloat16),
            pltpu.VMEM((n_col - 1, block, width), jnp.bfloat16),
            pltpu.SemaphoreType.DMA((4,)),
            pltpu.SemaphoreType.DMA((4,)),
            pltpu.SemaphoreType.DMA((n_col - 1,)),
            pltpu.SemaphoreType.DMA((n_col - 1,)),
        ],
        compiler_params=pltpu.CompilerParams(
            collective_id=0, has_side_effects=True, vmem_limit_bytes=52 << 20
        ),
    )(*pieces, weight, dense)


def general_body(features, weight, tiles, tile_rows, tile_cols, counts):
    feature_width = weight.shape[1]
    product_rows = jnp.dot(features, weight, preferred_element_type=jnp.float32).astype(
        jnp.bfloat16
    )
    gathered = lax.all_gather(product_rows, "row", axis=0, tiled=True)
    column_table = gathered.reshape(gathered.shape[0] // TILE, TILE, feature_width)
    row_tiles = lax.axis_size("col") * features.shape[0] // TILE
    slot_count = tile_rows.shape[2]
    block_size = min(64, slot_count)
    half_block = block_size // 2
    passes = slot_count // block_size
    pair_list = tiles[0, 0]
    row_list = tile_rows[0, 0]
    col_list = tile_cols[0, 0]
    live_count = counts[0, 0]
    block_slots = jnp.arange(block_size, dtype=jnp.int32)

    def add_block(block_index, total):
        first = block_index * block_size
        pair_block = lax.dynamic_slice_in_dim(pair_list, block_index * half_block, half_block, 0)
        pair_block = pair_block.reshape(half_block, TILE, 2, TILE)
        row_block = lax.dynamic_slice_in_dim(row_list, first, block_size, 0)
        col_block = lax.dynamic_slice_in_dim(col_list, first, block_size, 0)
        picked = column_table[col_block].reshape(half_block, 2, TILE, feature_width)
        terms = jnp.einsum(
            "qajb,qjbf->qjaf", pair_block, picked, preferred_element_type=jnp.float32
        )
        terms = terms.reshape(block_size, TILE, feature_width)
        in_use = (first + block_slots < live_count).astype(jnp.float32)
        terms = terms * in_use[:, None, None]
        return total.at[row_block].add(terms)

    zero_total = jnp.zeros((row_tiles, TILE, feature_width), jnp.float32)
    total = lax.fori_loop(0, passes, add_block, zero_total)
    partial_value = total.reshape(row_tiles * TILE, feature_width)
    own_rows = lax.psum_scatter(partial_value, "col", scatter_dimension=0, tiled=True)
    return jnp.maximum(own_rows, 0.0).astype(jnp.bfloat16)


def solution(mesh):
    n_row, n_col = mesh.shape["row"], mesh.shape["col"]
    fast = (n_row, n_col) == (8, 4)
    body = functools.partial(fast_body, n_row, n_col) if fast else general_body
    return jax.shard_map(
        body,
        mesh=mesh,
        in_specs=(
            P(("row", "col"), None),
            P(),
            P("row", "col", None, None, None),
            P("row", "col", None),
            P("row", "col", None),
            P("row", "col"),
        ),
        out_specs=P(("row", "col"), None),
        check_vma=False,
    )
```

```python
import functools

import jax
import jax.numpy as jnp
from jax import lax
from jax.experimental import pallas as pl
from jax.experimental.pallas import tpu as pltpu
from jax.sharding import PartitionSpec as P

TILE = 64
MESH = pl.DeviceIdType.MESH
CHUNKS = 8
GROUP = 8


def densify_kernel(
    counts, rows_hbm, cols_hbm, tiles_ref, dense_ref, rows, cols, tile_buf, acc, rounded,
    sems, index_sems, out_sems,
):
    pairs = tiles_ref.shape[2]
    per_chunk = pairs // CHUNKS
    index_copies = []
    for k, (src, dst) in enumerate(((rows_hbm, rows), (cols_hbm, cols))):
        copy = pltpu.make_async_copy(src, dst, index_sems.at[k])
        copy.start()
        index_copies.append(copy)
    copies = []
    for k in range(CHUNKS):
        part = pl.ds(k * per_chunk, per_chunk)
        copy = pltpu.make_async_copy(tiles_ref.at[0, 0, part], tile_buf.at[part], sems.at[k])
        copy.start()
        copies.append(copy)
    col_pairs = rounded.shape[0]
    row_tiles = rounded.shape[1] // TILE
    octets = TILE // 16
    col_octets = row_tiles * octets
    spare = 2 * col_pairs * col_octets

    @pl.loop(0, 2 * col_pairs)
    def _(i):
        zeros = jnp.zeros((col_octets, *acc.shape[1:]), acc.dtype)
        acc[pl.ds(i * col_octets, col_octets)] = zeros

    acc[spare:] = jnp.zeros((octets, *acc.shape[1:]), acc.dtype)
    for copy in index_copies:
        copy.wait()
    live = counts[0, 0]
    live_pairs = (live + 1) // 2
    low = lax.broadcasted_iota(jnp.int32, (TILE // 2, 2 * TILE), 1) < TILE

    for k in range(CHUNKS):
        copies[k].wait()
        first = k * per_chunk
        groups = jnp.clip((live_pairs - first + GROUP - 1) // GROUP, 0, per_chunk // GROUP)

        @pl.loop(0, groups)
        def _(g):
            start = first + g * GROUP
            work = []
            for j in range(GROUP):
                pair = tile_buf[start + j].astype(jnp.float32)
                turned = pltpu.roll(pair, TILE, 1)
                upper, lower = slice(0, TILE // 2), slice(TILE // 2, TILE)
                even = jnp.where(low, pair[upper], turned[lower])
                odd = jnp.where(low, turned[upper], pair[lower])
                work.append((even.reshape(octets, 8, 2 * TILE), odd.reshape(octets, 8, 2 * TILE)))
            for j in range(GROUP):
                p = 2 * (start + j)
                term0, term1 = work[j]
                place0 = cols[0, 0, p] * col_octets + rows[0, 0, p] * octets
                place1 = cols[0, 0, p + 1] * col_octets + rows[0, 0, p + 1] * octets
                place0 = jnp.where(p < live, place0, spare)
                place1 = jnp.where(p + 1 < live, place1, spare)
                at0 = pl.ds(place0, octets)
                at1 = pl.ds(place1, octets)
                again = term0 * jnp.where(place0 == place1, 1.0, 0.0)
                sum0 = acc[at0] + term0
                sum1 = acc[at1] + (term1 + again)
                acc[at0] = sum0
                acc[at1] = sum1

    out_copies = []
    for i in range(col_pairs):
        even, odd = (
            acc[c * col_octets : (c + 1) * col_octets].reshape(row_tiles * TILE // 2, 2 * TILE)
            for c in (2 * i, 2 * i + 1)
        )
        left = lax.broadcasted_iota(jnp.int32, even.shape, 1) < TILE
        upper = jnp.where(left, even, pltpu.roll(odd, TILE, 1))
        lower = jnp.where(left, pltpu.roll(even, TILE, 1), odd)
        halves = [x.reshape(row_tiles, TILE // 2, 2 * TILE) for x in (upper, lower)]
        block = jnp.concatenate(halves, axis=1).reshape(rounded.shape[1:])
        rounded[i] = block.astype(rounded.dtype)
        copy = pltpu.make_async_copy(rounded.at[i], dense_ref.at[i], out_sems.at[i])
        copy.start()
        out_copies.append(copy)
    for copy in out_copies:
        copy.wait()


def densify(counts, rows, cols, tiles, row_tiles, col_tiles):
    shape = (col_tiles // 2, row_tiles * TILE, 2 * TILE)
    hbm = pl.BlockSpec(memory_space=pltpu.HBM)
    return pl.pallas_call(
        densify_kernel,
        out_shape=jax.ShapeDtypeStruct(shape, jnp.bfloat16),
        in_specs=[pl.BlockSpec(memory_space=pltpu.VMEM)] + [hbm] * 3,
        out_specs=hbm,
        scratch_shapes=[
            pltpu.SMEM(rows.shape, jnp.int32),
            pltpu.SMEM(cols.shape, jnp.int32),
            pltpu.VMEM(tiles.shape[2:], tiles.dtype),
            pltpu.VMEM((shape[0] * shape[1] // 8 + TILE // 16, 8, shape[2]), jnp.float32),
            pltpu.VMEM(shape, jnp.bfloat16),
            pltpu.SemaphoreType.DMA((CHUNKS,)),
            pltpu.SemaphoreType.DMA((2,)),
            pltpu.SemaphoreType.DMA((shape[0],)),
        ],
        compiler_params=pltpu.CompilerParams(vmem_limit_bytes=61 << 20),
        cost_estimate=pl.CostEstimate(
            flops=5_000_000_000, bytes_accessed=2 * tiles.size, transcendentals=0
        ),
    )(counts, rows, cols, tiles)


def flip(index, mask, n):
    out, bit = 0, 1
    while bit < n:
        have = (index // bit) % 2
        out = out + bit * ((1 - have) if mask & bit else have)
        bit *= 2
    return out


def combine_kernel(
    n_row, n_col, own_ref, x_ref, y_ref, across_ref, weight_ref, dense_hbm, out_ref,
    dense_ref, dense_sem, table, send, recv, gather_send, gather_recv, send_sems, recv_sems,
):
    me_row, me = lax.axis_index("row"), lax.axis_index("col")
    block = out_ref.shape[0]
    barrier = pltpu.get_barrier_semaphore()
    buddy = flip(me_row, 1, n_row)
    pl.semaphore_signal(barrier, inc=1, device_id=(buddy, me), device_id_type=MESH)
    for j in range(1, n_col):
        pl.semaphore_signal(
            barrier, inc=1, device_id=(me_row, (me + j) % n_col), device_id_type=MESH
        )
    dense_copy = pltpu.make_async_copy(dense_hbm, dense_ref, dense_sem.at[0])
    dense_copy.start()

    def rows_of(source):
        return pl.ds(pl.multiple_of(source * block, block), block)

    weight = weight_ref[...]
    sources = [flip(me_row, m, n_row) for m in (0, 2, 4, 6)]
    for source, ref in zip(sources, (own_ref, x_ref, y_ref, across_ref)):
        product = jnp.dot(ref[...], weight, preferred_element_type=jnp.float32)
        table[rows_of(source)] = product.astype(table.dtype)
    pl.semaphore_wait(barrier, n_col)

    pieces = []
    for k, source in enumerate(sources):
        part = table.at[rows_of(source)]
        copy = pltpu.make_async_remote_copy(
            src_ref=part,
            dst_ref=part,
            send_sem=gather_send.at[k],
            recv_sem=gather_recv.at[k],
            device_id=(buddy, me),
            device_id_type=MESH,
        )
        copy.start()
        pieces.append(copy)
    dense_copy.wait()
    for copy in pieces:
        copy.wait_recv()

    def partial(owner):
        at = rows_of(owner)
        left = jnp.concatenate([dense_ref[i, at] for i in range(dense_ref.shape[0])], axis=1)
        return jnp.dot(left, table[...], preferred_element_type=jnp.float32)

    copies = []
    for j in (2, 1, 3):
        peer = (me + j) % n_col
        send[j - 1] = partial(peer).astype(send.dtype)
        copy = pltpu.make_async_remote_copy(
            src_ref=send.at[j - 1],
            dst_ref=recv.at[j - 1],
            send_sem=send_sems.at[j - 1],
            recv_sem=recv_sems.at[j - 1],
            device_id=(me_row, peer),
            device_id_type=MESH,
        )
        copy.start()
        copies.append((j, copy))
    total = partial(me)
    for j, copy in copies:
        copy.wait_recv()
        total = total + recv[j - 1].astype(jnp.float32)
    out_ref[...] = jnp.maximum(total, 0.0).astype(out_ref.dtype)
    for copy in pieces:
        copy.wait_send()
    for j, copy in copies:
        copy.wait_send()


def fast_body(n_row, n_col, features, weight, tiles, tile_rows, tile_cols, counts):
    block, width = features.shape
    pieces = [features]
    for m in (2, 4, 6):
        pieces.append(lax.ppermute(features, "row", [(i, i ^ m) for i in range(n_row)]))
    dense = densify(
        counts, tile_rows, tile_cols, tiles, n_col * block // TILE, n_row * block // TILE
    )
    vmem = pl.BlockSpec(memory_space=pltpu.VMEM)
    return pl.pallas_call(
        functools.partial(combine_kernel, n_row, n_col),
        out_shape=jax.ShapeDtypeStruct((block, width), jnp.bfloat16),
        in_specs=[vmem] * 5 + [pl.BlockSpec(memory_space=pltpu.HBM)],
        out_specs=vmem,
        scratch_shapes=[
            pltpu.VMEM(dense.shape, dense.dtype),
            pltpu.SemaphoreType.DMA((1,)),
            pltpu.VMEM((n_row * block, width), jnp.bfloat16),
            pltpu.VMEM((n_col - 1, block, width), jnp.bfloat16),
            pltpu.VMEM((n_col - 1, block, width), jnp.bfloat16),
            pltpu.SemaphoreType.DMA((4,)),
            pltpu.SemaphoreType.DMA((4,)),
            pltpu.SemaphoreType.DMA((n_col - 1,)),
            pltpu.SemaphoreType.DMA((n_col - 1,)),
        ],
        compiler_params=pltpu.CompilerParams(
            collective_id=0, has_side_effects=True, vmem_limit_bytes=52 << 20
        ),
    )(*pieces, weight, dense)


def general_body(features, weight, tiles, tile_rows, tile_cols, counts):
    feature_width = weight.shape[1]
    product_rows = jnp.dot(features, weight, preferred_element_type=jnp.float32).astype(
        jnp.bfloat16
    )
    gathered = lax.all_gather(product_rows, "row", axis=0, tiled=True)
    column_table = gathered.reshape(gathered.shape[0] // TILE, TILE, feature_width)
    row_tiles = lax.axis_size("col") * features.shape[0] // TILE
    slot_count = tile_rows.shape[2]
    block_size = min(64, slot_count)
    half_block = block_size // 2
    passes = slot_count // block_size
    pair_list = tiles[0, 0]
    row_list = tile_rows[0, 0]
    col_list = tile_cols[0, 0]
    live_count = counts[0, 0]
    block_slots = jnp.arange(block_size, dtype=jnp.int32)

    def add_block(block_index, total):
        first = block_index * block_size
        pair_block = lax.dynamic_slice_in_dim(pair_list, block_index * half_block, half_block, 0)
        pair_block = pair_block.reshape(half_block, TILE, 2, TILE)
        row_block = lax.dynamic_slice_in_dim(row_list, first, block_size, 0)
        col_block = lax.dynamic_slice_in_dim(col_list, first, block_size, 0)
        picked = column_table[col_block].reshape(half_block, 2, TILE, feature_width)
        terms = jnp.einsum(
            "qajb,qjbf->qjaf", pair_block, picked, preferred_element_type=jnp.float32
        )
        terms = terms.reshape(block_size, TILE, feature_width)
        in_use = (first + block_slots < live_count).astype(jnp.float32)
        terms = terms * in_use[:, None, None]
        return total.at[row_block].add(terms)

    zero_total = jnp.zeros((row_tiles, TILE, feature_width), jnp.float32)
    total = lax.fori_loop(0, passes, add_block, zero_total)
    partial_value = total.reshape(row_tiles * TILE, feature_width)
    own_rows = lax.psum_scatter(partial_value, "col", scatter_dimension=0, tiled=True)
    return jnp.maximum(own_rows, 0.0).astype(jnp.bfloat16)


def solution(mesh):
    n_row, n_col = mesh.shape["row"], mesh.shape["col"]
    fast = (n_row, n_col) == (8, 4)
    body = functools.partial(fast_body, n_row, n_col) if fast else general_body
    return jax.shard_map(
        body,
        mesh=mesh,
        in_specs=(
            P(("row", "col"), None),
            P(),
            P("row", "col", None, None, None),
            P("row", "col", None),
            P("row", "col", None),
            P("row", "col"),
        ),
        out_specs=P(("row", "col"), None),
        check_vma=False,
    )
```

```python
import functools

import jax
import jax.numpy as jnp
from jax import lax
from jax.experimental import pallas as pl
from jax.experimental.pallas import tpu as pltpu
from jax.sharding import PartitionSpec as P

TILE = 64
MESH = pl.DeviceIdType.MESH
CHUNKS = 8
GROUP = 8


def densify_kernel(
    counts, rows_hbm, cols_hbm, tiles_ref, dense_ref, rows, cols, tile_buf, acc, rounded,
    sems, index_sems, out_sems,
):
    pairs = tiles_ref.shape[2]
    per_chunk = pairs // CHUNKS
    index_copies = []
    for k, (src, dst) in enumerate(((rows_hbm, rows), (cols_hbm, cols))):
        copy = pltpu.make_async_copy(src, dst, index_sems.at[k])
        copy.start()
        index_copies.append(copy)
    copies = []
    for k in range(CHUNKS):
        part = pl.ds(k * per_chunk, per_chunk)
        copy = pltpu.make_async_copy(tiles_ref.at[0, 0, part], tile_buf.at[part], sems.at[k])
        copy.start()
        copies.append(copy)
    col_pairs = rounded.shape[0]
    row_tiles = rounded.shape[1] // TILE
    octets = TILE // 16
    col_octets = row_tiles * octets
    spare = 2 * col_pairs * col_octets

    @pl.loop(0, 2 * col_pairs)
    def _(i):
        zeros = jnp.zeros((col_octets, *acc.shape[1:]), acc.dtype)
        acc[pl.ds(i * col_octets, col_octets)] = zeros

    acc[spare:] = jnp.zeros((octets, *acc.shape[1:]), acc.dtype)
    for copy in index_copies:
        copy.wait()
    live = counts[0, 0]
    live_pairs = (live + 1) // 2
    low = lax.broadcasted_iota(jnp.int32, (TILE // 2, 2 * TILE), 1) < TILE

    for k in range(CHUNKS):
        copies[k].wait()
        first = k * per_chunk
        groups = jnp.clip((live_pairs - first + GROUP - 1) // GROUP, 0, per_chunk // GROUP)

        @pl.loop(0, groups)
        def _(g):
            start = first + g * GROUP
            work = []
            for j in range(GROUP):
                pair = tile_buf[start + j].astype(jnp.float32)
                turned = pltpu.roll(pair, TILE, 1)
                upper, lower = slice(0, TILE // 2), slice(TILE // 2, TILE)
                even = jnp.where(low, pair[upper], turned[lower])
                odd = jnp.where(low, turned[upper], pair[lower])
                work.append((even.reshape(octets, 8, 2 * TILE), odd.reshape(octets, 8, 2 * TILE)))
            for j in range(GROUP):
                p = 2 * (start + j)
                term0, term1 = work[j]
                place0 = cols[0, 0, p] * col_octets + rows[0, 0, p] * octets
                place1 = cols[0, 0, p + 1] * col_octets + rows[0, 0, p + 1] * octets
                place0 = jnp.where(p < live, place0, spare)
                place1 = jnp.where(p + 1 < live, place1, spare)
                at0 = pl.ds(place0, octets)
                at1 = pl.ds(place1, octets)
                again = term0 * jnp.where(place0 == place1, 1.0, 0.0)
                sum0 = acc[at0] + term0
                sum1 = acc[at1] + (term1 + again)
                acc[at0] = sum0
                acc[at1] = sum1

    out_copies = []
    for i in range(col_pairs):
        even, odd = (
            acc[c * col_octets : (c + 1) * col_octets].reshape(row_tiles * TILE // 2, 2 * TILE)
            for c in (2 * i, 2 * i + 1)
        )
        left = lax.broadcasted_iota(jnp.int32, even.shape, 1) < TILE
        upper = jnp.where(left, even, pltpu.roll(odd, TILE, 1))
        lower = jnp.where(left, pltpu.roll(even, TILE, 1), odd)
        halves = [x.reshape(row_tiles, TILE // 2, 2 * TILE) for x in (upper, lower)]
        block = jnp.concatenate(halves, axis=1).reshape(rounded.shape[1:])
        rounded[i] = block.astype(rounded.dtype)
        copy = pltpu.make_async_copy(rounded.at[i], dense_ref.at[i], out_sems.at[i])
        copy.start()
        out_copies.append(copy)
    for copy in out_copies:
        copy.wait()


def densify(counts, rows, cols, tiles, row_tiles, col_tiles):
    shape = (col_tiles // 2, row_tiles * TILE, 2 * TILE)
    hbm = pl.BlockSpec(memory_space=pltpu.HBM)
    return pl.pallas_call(
        densify_kernel,
        out_shape=jax.ShapeDtypeStruct(shape, jnp.bfloat16),
        in_specs=[pl.BlockSpec(memory_space=pltpu.VMEM)] + [hbm] * 3,
        out_specs=hbm,
        scratch_shapes=[
            pltpu.SMEM(rows.shape, jnp.int32),
            pltpu.SMEM(cols.shape, jnp.int32),
            pltpu.VMEM(tiles.shape[2:], tiles.dtype),
            pltpu.VMEM((shape[0] * shape[1] // 8 + TILE // 16, 8, shape[2]), jnp.float32),
            pltpu.VMEM(shape, jnp.bfloat16),
            pltpu.SemaphoreType.DMA((CHUNKS,)),
            pltpu.SemaphoreType.DMA((2,)),
            pltpu.SemaphoreType.DMA((shape[0],)),
        ],
        compiler_params=pltpu.CompilerParams(vmem_limit_bytes=61 << 20),
        cost_estimate=pl.CostEstimate(
            flops=5_000_000_000, bytes_accessed=2 * tiles.size, transcendentals=0
        ),
    )(counts, rows, cols, tiles)


def flip(index, mask, n):
    out, bit = 0, 1
    while bit < n:
        have = (index // bit) % 2
        out = out + bit * ((1 - have) if mask & bit else have)
        bit *= 2
    return out


def combine_kernel(
    n_row, n_col, own_ref, x_ref, y_ref, across_ref, weight_ref, dense_hbm, out_ref,
    dense_ref, dense_sem, table, send, recv, gather_send, gather_recv, send_sems, recv_sems,
):
    me_row, me = lax.axis_index("row"), lax.axis_index("col")
    block = out_ref.shape[0]
    barrier = pltpu.get_barrier_semaphore()
    buddy = flip(me_row, 1, n_row)
    pl.semaphore_signal(barrier, inc=1, device_id=(buddy, me), device_id_type=MESH)
    for j in range(1, n_col):
        pl.semaphore_signal(
            barrier, inc=1, device_id=(me_row, (me + j) % n_col), device_id_type=MESH
        )
    dense_copy = pltpu.make_async_copy(dense_hbm, dense_ref, dense_sem.at[0])
    dense_copy.start()

    def rows_of(source):
        return pl.ds(pl.multiple_of(source * block, block), block)

    weight = weight_ref[...]
    sources = [flip(me_row, m, n_row) for m in (0, 2, 4, 6)]
    for source, ref in zip(sources, (own_ref, x_ref, y_ref, across_ref)):
        product = jnp.dot(ref[...], weight, preferred_element_type=jnp.float32)
        table[rows_of(source)] = product.astype(table.dtype)
    pl.semaphore_wait(barrier, n_col)

    pieces = []
    for k, source in enumerate(sources):
        part = table.at[rows_of(source)]
        copy = pltpu.make_async_remote_copy(
            src_ref=part,
            dst_ref=part,
            send_sem=gather_send.at[k],
            recv_sem=gather_recv.at[k],
            device_id=(buddy, me),
            device_id_type=MESH,
        )
        copy.start()
        pieces.append(copy)
    dense_copy.wait()
    for copy in pieces:
        copy.wait_recv()

    def partial(owner):
        at = rows_of(owner)
        left = jnp.concatenate([dense_ref[i, at] for i in range(dense_ref.shape[0])], axis=1)
        return jnp.dot(left, table[...], preferred_element_type=jnp.float32)

    def copy_to(k, slot, target):
        return pltpu.make_async_remote_copy(
            src_ref=send.at[k],
            dst_ref=recv.at[slot],
            send_sem=send_sems.at[k],
            recv_sem=recv_sems.at[slot],
            device_id=(me_row, target),
            device_id_type=MESH,
        )

    def fire(k, slot, target, value):
        send[k] = value.astype(send.dtype)
        copy = copy_to(k, slot, target)
        copy.start()
        return copy

    def arrived(slot, any_peer):
        copy_to(0, slot, any_peer).wait_recv()
        return recv[slot].astype(jnp.float32)

    def finish(copies, slots, any_peer):
        total = partial(me)
        for slot in slots:
            total = total + arrived(slot, any_peer)
        out_ref[...] = jnp.maximum(total, 0.0).astype(out_ref.dtype)
        for copy in copies:
            copy.wait_send()

    last = n_col - 1
    is_end = me % last == 0

    @pl.when(is_end)
    def _():
        near = 1 + me // last
        far, opposite = last - near, last - me
        copies = [
            fire(0, 3, near, partial(opposite)),
            fire(1, 1, far, partial(far)),
            fire(2, 0, near, partial(near)),
        ]
        finish(copies, (0, 1), near)

    @pl.when(jnp.logical_not(is_end))
    def _():
        near = last * (me - 1)
        other, opposite = last - me, last - near
        copies = [fire(0, 2, other, partial(other)), fire(1, 0, near, partial(near))]
        merged = partial(opposite)
        copies.append(fire(2, 1, opposite, merged + arrived(3, near)))
        finish(copies, (2, 1, 0), near)

    for copy in pieces:
        copy.wait_send()


def fast_body(n_row, n_col, features, weight, tiles, tile_rows, tile_cols, counts):
    block, width = features.shape
    pieces = [features]
    for m in (2, 4, 6):
        pieces.append(lax.ppermute(features, "row", [(i, i ^ m) for i in range(n_row)]))
    dense = densify(
        counts, tile_rows, tile_cols, tiles, n_col * block // TILE, n_row * block // TILE
    )
    vmem = pl.BlockSpec(memory_space=pltpu.VMEM)
    return pl.pallas_call(
        functools.partial(combine_kernel, n_row, n_col),
        out_shape=jax.ShapeDtypeStruct((block, width), jnp.bfloat16),
        in_specs=[vmem] * 5 + [pl.BlockSpec(memory_space=pltpu.HBM)],
        out_specs=vmem,
        scratch_shapes=[
            pltpu.VMEM(dense.shape, dense.dtype),
            pltpu.SemaphoreType.DMA((1,)),
            pltpu.VMEM((n_row * block, width), jnp.bfloat16),
            pltpu.VMEM((n_col - 1, block, width), jnp.bfloat16),
            pltpu.VMEM((n_col, block, width), jnp.bfloat16),
            pltpu.SemaphoreType.DMA((4,)),
            pltpu.SemaphoreType.DMA((4,)),
            pltpu.SemaphoreType.DMA((n_col - 1,)),
            pltpu.SemaphoreType.DMA((n_col,)),
        ],
        compiler_params=pltpu.CompilerParams(
            collective_id=0, has_side_effects=True, vmem_limit_bytes=52 << 20
        ),
    )(*pieces, weight, dense)


def general_body(features, weight, tiles, tile_rows, tile_cols, counts):
    feature_width = weight.shape[1]
    product_rows = jnp.dot(features, weight, preferred_element_type=jnp.float32).astype(
        jnp.bfloat16
    )
    gathered = lax.all_gather(product_rows, "row", axis=0, tiled=True)
    column_table = gathered.reshape(gathered.shape[0] // TILE, TILE, feature_width)
    row_tiles = lax.axis_size("col") * features.shape[0] // TILE
    slot_count = tile_rows.shape[2]
    block_size = min(64, slot_count)
    half_block = block_size // 2
    passes = slot_count // block_size
    pair_list = tiles[0, 0]
    row_list = tile_rows[0, 0]
    col_list = tile_cols[0, 0]
    live_count = counts[0, 0]
    block_slots = jnp.arange(block_size, dtype=jnp.int32)

    def add_block(block_index, total):
        first = block_index * block_size
        pair_block = lax.dynamic_slice_in_dim(pair_list, block_index * half_block, half_block, 0)
        pair_block = pair_block.reshape(half_block, TILE, 2, TILE)
        row_block = lax.dynamic_slice_in_dim(row_list, first, block_size, 0)
        col_block = lax.dynamic_slice_in_dim(col_list, first, block_size, 0)
        picked = column_table[col_block].reshape(half_block, 2, TILE, feature_width)
        terms = jnp.einsum(
            "qajb,qjbf->qjaf", pair_block, picked, preferred_element_type=jnp.float32
        )
        terms = terms.reshape(block_size, TILE, feature_width)
        in_use = (first + block_slots < live_count).astype(jnp.float32)
        terms = terms * in_use[:, None, None]
        return total.at[row_block].add(terms)

    zero_total = jnp.zeros((row_tiles, TILE, feature_width), jnp.float32)
    total = lax.fori_loop(0, passes, add_block, zero_total)
    partial_value = total.reshape(row_tiles * TILE, feature_width)
    own_rows = lax.psum_scatter(partial_value, "col", scatter_dimension=0, tiled=True)
    return jnp.maximum(own_rows, 0.0).astype(jnp.bfloat16)


def solution(mesh):
    n_row, n_col = mesh.shape["row"], mesh.shape["col"]
    fast = (n_row, n_col) == (8, 4)
    body = functools.partial(fast_body, n_row, n_col) if fast else general_body
    return jax.shard_map(
        body,
        mesh=mesh,
        in_specs=(
            P(("row", "col"), None),
            P(),
            P("row", "col", None, None, None),
            P("row", "col", None),
            P("row", "col", None),
            P("row", "col"),
        ),
        out_specs=P(("row", "col"), None),
        check_vma=False,
    )
```

```python
import functools

import jax
import jax.numpy as jnp
from jax import lax
from jax.experimental import pallas as pl
from jax.experimental.pallas import tpu as pltpu
from jax.sharding import PartitionSpec as P

TILE = 64
MESH = pl.DeviceIdType.MESH
CHUNKS = 8
GROUP = 8


def densify_kernel(
    counts, rows_hbm, cols_hbm, tiles_ref, dense_ref, rows, cols, tile_buf, acc, rounded,
    sems, index_sems, out_sems,
):
    pairs = tiles_ref.shape[2]
    per_chunk = pairs // CHUNKS
    index_copies = []
    for k, (src, dst) in enumerate(((rows_hbm, rows), (cols_hbm, cols))):
        copy = pltpu.make_async_copy(src, dst, index_sems.at[k])
        copy.start()
        index_copies.append(copy)
    copies = []
    for k in range(CHUNKS):
        part = pl.ds(k * per_chunk, per_chunk)
        copy = pltpu.make_async_copy(tiles_ref.at[0, 0, part], tile_buf.at[part], sems.at[k])
        copy.start()
        copies.append(copy)
    col_pairs = rounded.shape[0]
    row_tiles = rounded.shape[1] // TILE
    octets = TILE // 16
    col_octets = row_tiles * octets
    spare = 2 * col_pairs * col_octets

    @pl.loop(0, 2 * col_pairs)
    def _(i):
        zeros = jnp.zeros((col_octets, *acc.shape[1:]), acc.dtype)
        acc[pl.ds(i * col_octets, col_octets)] = zeros

    acc[spare:] = jnp.zeros((octets, *acc.shape[1:]), acc.dtype)
    for copy in index_copies:
        copy.wait()
    live = counts[0, 0]
    live_pairs = (live + 1) // 2
    low = lax.broadcasted_iota(jnp.int32, (TILE // 2, 2 * TILE), 1) < TILE

    for k in range(CHUNKS):
        copies[k].wait()
        first = k * per_chunk
        groups = jnp.clip((live_pairs - first + GROUP - 1) // GROUP, 0, per_chunk // GROUP)

        @pl.loop(0, groups)
        def _(g):
            start = first + g * GROUP
            for j in range(GROUP):
                pair = tile_buf[start + j].astype(jnp.float32)
                turned = pltpu.roll(pair, TILE, 1)
                upper, lower = slice(0, TILE // 2), slice(TILE // 2, TILE)
                even = jnp.where(low, pair[upper], turned[lower])
                odd = jnp.where(low, turned[upper], pair[lower])
                term0 = even.reshape(octets, 8, 2 * TILE)
                term1 = odd.reshape(octets, 8, 2 * TILE)
                p = 2 * (start + j)
                place0 = cols[0, 0, p] * col_octets + rows[0, 0, p] * octets
                place1 = cols[0, 0, p + 1] * col_octets + rows[0, 0, p + 1] * octets
                place0 = jnp.where(p < live, place0, spare)
                place1 = jnp.where(p + 1 < live, place1, spare)
                at0 = pl.ds(place0, octets)
                at1 = pl.ds(place1, octets)
                again = term0 * jnp.where(place0 == place1, 1.0, 0.0)
                sum0 = acc[at0] + term0
                sum1 = acc[at1] + (term1 + again)
                acc[at0] = sum0
                acc[at1] = sum1

    out_copies = []
    for i in range(col_pairs):
        even, odd = (
            acc[c * col_octets : (c + 1) * col_octets].reshape(row_tiles * TILE // 2, 2 * TILE)
            for c in (2 * i, 2 * i + 1)
        )
        left = lax.broadcasted_iota(jnp.int32, even.shape, 1) < TILE
        upper = jnp.where(left, even, pltpu.roll(odd, TILE, 1))
        lower = jnp.where(left, pltpu.roll(even, TILE, 1), odd)
        halves = [x.reshape(row_tiles, TILE // 2, 2 * TILE) for x in (upper, lower)]
        block = jnp.concatenate(halves, axis=1).reshape(rounded.shape[1:])
        rounded[i] = block.astype(rounded.dtype)
        copy = pltpu.make_async_copy(rounded.at[i], dense_ref.at[i], out_sems.at[i])
        copy.start()
        out_copies.append(copy)
    for copy in out_copies:
        copy.wait()


def densify(counts, rows, cols, tiles, row_tiles, col_tiles):
    shape = (col_tiles // 2, row_tiles * TILE, 2 * TILE)
    hbm = pl.BlockSpec(memory_space=pltpu.HBM)
    return pl.pallas_call(
        densify_kernel,
        out_shape=jax.ShapeDtypeStruct(shape, jnp.bfloat16),
        in_specs=[pl.BlockSpec(memory_space=pltpu.VMEM)] + [hbm] * 3,
        out_specs=hbm,
        scratch_shapes=[
            pltpu.SMEM(rows.shape, jnp.int32),
            pltpu.SMEM(cols.shape, jnp.int32),
            pltpu.VMEM(tiles.shape[2:], tiles.dtype),
            pltpu.VMEM((shape[0] * shape[1] // 8 + TILE // 16, 8, shape[2]), jnp.float32),
            pltpu.VMEM(shape, jnp.bfloat16),
            pltpu.SemaphoreType.DMA((CHUNKS,)),
            pltpu.SemaphoreType.DMA((2,)),
            pltpu.SemaphoreType.DMA((shape[0],)),
        ],
        compiler_params=pltpu.CompilerParams(vmem_limit_bytes=61 << 20),
        cost_estimate=pl.CostEstimate(
            flops=5_000_000_000, bytes_accessed=2 * tiles.size, transcendentals=0
        ),
    )(counts, rows, cols, tiles)


def flip(index, mask, n):
    out, bit = 0, 1
    while bit < n:
        have = (index // bit) % 2
        out = out + bit * ((1 - have) if mask & bit else have)
        bit *= 2
    return out


def combine_kernel(
    n_row, n_col, own_ref, x_ref, y_ref, across_ref, weight_ref, dense_hbm, out_ref,
    dense_ref, dense_sem, table, send, recv, gather_send, gather_recv, send_sems, recv_sems,
):
    me_row, me = lax.axis_index("row"), lax.axis_index("col")
    block = out_ref.shape[0]
    barrier = pltpu.get_barrier_semaphore()
    buddy = flip(me_row, 1, n_row)
    pl.semaphore_signal(barrier, inc=1, device_id=(buddy, me), device_id_type=MESH)
    for j in range(1, n_col):
        pl.semaphore_signal(
            barrier, inc=1, device_id=(me_row, (me + j) % n_col), device_id_type=MESH
        )
    dense_copy = pltpu.make_async_copy(dense_hbm, dense_ref, dense_sem.at[0])
    dense_copy.start()

    def rows_of(source):
        return pl.ds(pl.multiple_of(source * block, block), block)

    weight = weight_ref[...]
    sources = [flip(me_row, m, n_row) for m in (0, 2, 4, 6)]
    for source, ref in zip(sources, (own_ref, x_ref, y_ref, across_ref)):
        product = jnp.dot(ref[...], weight, preferred_element_type=jnp.float32)
        table[rows_of(source)] = product.astype(table.dtype)
    pl.semaphore_wait(barrier, n_col)

    pieces = []
    for k, source in enumerate(sources):
        part = table.at[rows_of(source)]
        copy = pltpu.make_async_remote_copy(
            src_ref=part,
            dst_ref=part,
            send_sem=gather_send.at[k],
            recv_sem=gather_recv.at[k],
            device_id=(buddy, me),
            device_id_type=MESH,
        )
        copy.start()
        pieces.append(copy)
    dense_copy.wait()
    for copy in pieces:
        copy.wait_recv()

    def partial(owner):
        at = rows_of(owner)
        left = jnp.concatenate([dense_ref[i, at] for i in range(dense_ref.shape[0])], axis=1)
        return jnp.dot(left, table[...], preferred_element_type=jnp.float32)

    copies = []
    for j in (2, 1, 3):
        peer = (me + j) % n_col
        send[j - 1] = partial(peer).astype(send.dtype)
        copy = pltpu.make_async_remote_copy(
            src_ref=send.at[j - 1],
            dst_ref=recv.at[j - 1],
            send_sem=send_sems.at[j - 1],
            recv_sem=recv_sems.at[j - 1],
            device_id=(me_row, peer),
            device_id_type=MESH,
        )
        copy.start()
        copies.append((j, copy))
    total = partial(me)
    for j, copy in copies:
        copy.wait_recv()
        total = total + recv[j - 1].astype(jnp.float32)
    out_ref[...] = jnp.maximum(total, 0.0).astype(out_ref.dtype)
    for copy in pieces:
        copy.wait_send()
    for j, copy in copies:
        copy.wait_send()


def fast_body(n_row, n_col, features, weight, tiles, tile_rows, tile_cols, counts):
    block, width = features.shape
    pieces = [features]
    for m in (2, 4, 6):
        pieces.append(lax.ppermute(features, "row", [(i, i ^ m) for i in range(n_row)]))
    dense = densify(
        counts, tile_rows, tile_cols, tiles, n_col * block // TILE, n_row * block // TILE
    )
    vmem = pl.BlockSpec(memory_space=pltpu.VMEM)
    return pl.pallas_call(
        functools.partial(combine_kernel, n_row, n_col),
        out_shape=jax.ShapeDtypeStruct((block, width), jnp.bfloat16),
        in_specs=[vmem] * 5 + [pl.BlockSpec(memory_space=pltpu.HBM)],
        out_specs=vmem,
        scratch_shapes=[
            pltpu.VMEM(dense.shape, dense.dtype),
            pltpu.SemaphoreType.DMA((1,)),
            pltpu.VMEM((n_row * block, width), jnp.bfloat16),
            pltpu.VMEM((n_col - 1, block, width), jnp.bfloat16),
            pltpu.VMEM((n_col - 1, block, width), jnp.bfloat16),
            pltpu.SemaphoreType.DMA((4,)),
            pltpu.SemaphoreType.DMA((4,)),
            pltpu.SemaphoreType.DMA((n_col - 1,)),
            pltpu.SemaphoreType.DMA((n_col - 1,)),
        ],
        compiler_params=pltpu.CompilerParams(
            collective_id=0, has_side_effects=True, vmem_limit_bytes=52 << 20
        ),
    )(*pieces, weight, dense)


def general_body(features, weight, tiles, tile_rows, tile_cols, counts):
    feature_width = weight.shape[1]
    product_rows = jnp.dot(features, weight, preferred_element_type=jnp.float32).astype(
        jnp.bfloat16
    )
    gathered = lax.all_gather(product_rows, "row", axis=0, tiled=True)
    column_table = gathered.reshape(gathered.shape[0] // TILE, TILE, feature_width)
    row_tiles = lax.axis_size("col") * features.shape[0] // TILE
    slot_count = tile_rows.shape[2]
    block_size = min(64, slot_count)
    half_block = block_size // 2
    passes = slot_count // block_size
    pair_list = tiles[0, 0]
    row_list = tile_rows[0, 0]
    col_list = tile_cols[0, 0]
    live_count = counts[0, 0]
    block_slots = jnp.arange(block_size, dtype=jnp.int32)

    def add_block(block_index, total):
        first = block_index * block_size
        pair_block = lax.dynamic_slice_in_dim(pair_list, block_index * half_block, half_block, 0)
        pair_block = pair_block.reshape(half_block, TILE, 2, TILE)
        row_block = lax.dynamic_slice_in_dim(row_list, first, block_size, 0)
        col_block = lax.dynamic_slice_in_dim(col_list, first, block_size, 0)
        picked = column_table[col_block].reshape(half_block, 2, TILE, feature_width)
        terms = jnp.einsum(
            "qajb,qjbf->qjaf", pair_block, picked, preferred_element_type=jnp.float32
        )
        terms = terms.reshape(block_size, TILE, feature_width)
        in_use = (first + block_slots < live_count).astype(jnp.float32)
        terms = terms * in_use[:, None, None]
        return total.at[row_block].add(terms)

    zero_total = jnp.zeros((row_tiles, TILE, feature_width), jnp.float32)
    total = lax.fori_loop(0, passes, add_block, zero_total)
    partial_value = total.reshape(row_tiles * TILE, feature_width)
    own_rows = lax.psum_scatter(partial_value, "col", scatter_dimension=0, tiled=True)
    return jnp.maximum(own_rows, 0.0).astype(jnp.bfloat16)


def solution(mesh):
    n_row, n_col = mesh.shape["row"], mesh.shape["col"]
    fast = (n_row, n_col) == (8, 4)
    body = functools.partial(fast_body, n_row, n_col) if fast else general_body
    return jax.shard_map(
        body,
        mesh=mesh,
        in_specs=(
            P(("row", "col"), None),
            P(),
            P("row", "col", None, None, None),
            P("row", "col", None),
            P("row", "col", None),
            P("row", "col"),
        ),
        out_specs=P(("row", "col"), None),
        check_vma=False,
    )
```

```python
import functools

import jax
import jax.numpy as jnp
from jax import lax
from jax.experimental import pallas as pl
from jax.experimental.pallas import tpu as pltpu
from jax.sharding import PartitionSpec as P

TILE = 64
MESH = pl.DeviceIdType.MESH
CHUNKS = 8
GROUP = 8


def densify_kernel(
    counts, rows_hbm, cols_hbm, tiles_ref, dense_ref, rows, cols, tile_buf, acc, odd_acc, rounded,
    sems, index_sems, out_sems,
):
    pairs = tiles_ref.shape[2]
    per_chunk = pairs // CHUNKS
    index_copies = []
    for k, (src, dst) in enumerate(((rows_hbm, rows), (cols_hbm, cols))):
        copy = pltpu.make_async_copy(src, dst, index_sems.at[k])
        copy.start()
        index_copies.append(copy)
    copies = []
    for k in range(CHUNKS):
        part = pl.ds(k * per_chunk, per_chunk)
        copy = pltpu.make_async_copy(tiles_ref.at[0, 0, part], tile_buf.at[part], sems.at[k])
        copy.start()
        copies.append(copy)
    col_pairs = rounded.shape[0]
    row_tiles = rounded.shape[1] // TILE
    octets = TILE // 16
    col_octets = row_tiles * octets
    spare = 2 * col_pairs * col_octets

    @pl.loop(0, 2 * col_pairs)
    def _(i):
        zeros = jnp.zeros((col_octets, *acc.shape[1:]), acc.dtype)
        acc[pl.ds(i * col_octets, col_octets)] = zeros
        odd_acc[pl.ds(i * col_octets, col_octets)] = zeros

    acc[spare:] = jnp.zeros((octets, *acc.shape[1:]), acc.dtype)
    odd_acc[spare:] = jnp.zeros((octets, *acc.shape[1:]), acc.dtype)
    for copy in index_copies:
        copy.wait()
    live = counts[0, 0]
    live_pairs = (live + 1) // 2
    low = lax.broadcasted_iota(jnp.int32, (TILE // 2, 2 * TILE), 1) < TILE

    for k in range(CHUNKS):
        copies[k].wait()
        first = k * per_chunk
        groups = jnp.clip((live_pairs - first + GROUP - 1) // GROUP, 0, per_chunk // GROUP)

        @pl.loop(0, groups)
        def _(g):
            start = first + g * GROUP
            for j in range(GROUP):
                pair = tile_buf[start + j].astype(jnp.float32)
                turned = pltpu.roll(pair, TILE, 1)
                upper, lower = slice(0, TILE // 2), slice(TILE // 2, TILE)
                even = jnp.where(low, pair[upper], turned[lower])
                odd = jnp.where(low, turned[upper], pair[lower])
                term0 = even.reshape(octets, 8, 2 * TILE)
                term1 = odd.reshape(octets, 8, 2 * TILE)
                p = 2 * (start + j)
                place0 = cols[0, 0, p] * col_octets + rows[0, 0, p] * octets
                place1 = cols[0, 0, p + 1] * col_octets + rows[0, 0, p + 1] * octets
                place0 = jnp.where(p < live, place0, spare)
                place1 = jnp.where(p + 1 < live, place1, spare)
                at0 = pl.ds(place0, octets)
                at1 = pl.ds(place1, octets)
                acc[at0] += term0
                odd_acc[at1] += term1

    out_copies = []
    for i in range(col_pairs):
        even, odd = (
            (
                acc[c * col_octets : (c + 1) * col_octets]
                + odd_acc[c * col_octets : (c + 1) * col_octets]
            ).reshape(row_tiles * TILE // 2, 2 * TILE)
            for c in (2 * i, 2 * i + 1)
        )
        left = lax.broadcasted_iota(jnp.int32, even.shape, 1) < TILE
        upper = jnp.where(left, even, pltpu.roll(odd, TILE, 1))
        lower = jnp.where(left, pltpu.roll(even, TILE, 1), odd)
        halves = [x.reshape(row_tiles, TILE // 2, 2 * TILE) for x in (upper, lower)]
        block = jnp.concatenate(halves, axis=1).reshape(rounded.shape[1:])
        rounded[i] = block.astype(rounded.dtype)
        copy = pltpu.make_async_copy(rounded.at[i], dense_ref.at[i], out_sems.at[i])
        copy.start()
        out_copies.append(copy)
    for copy in out_copies:
        copy.wait()


def densify(counts, rows, cols, tiles, row_tiles, col_tiles):
    shape = (col_tiles // 2, row_tiles * TILE, 2 * TILE)
    hbm = pl.BlockSpec(memory_space=pltpu.HBM)
    return pl.pallas_call(
        densify_kernel,
        out_shape=jax.ShapeDtypeStruct(shape, jnp.bfloat16),
        in_specs=[pl.BlockSpec(memory_space=pltpu.VMEM)] + [hbm] * 3,
        out_specs=hbm,
        scratch_shapes=[
            pltpu.SMEM(rows.shape, jnp.int32),
            pltpu.SMEM(cols.shape, jnp.int32),
            pltpu.VMEM(tiles.shape[2:], tiles.dtype),
            pltpu.VMEM((shape[0] * shape[1] // 8 + TILE // 16, 8, shape[2]), jnp.float32),
            pltpu.VMEM((shape[0] * shape[1] // 8 + TILE // 16, 8, shape[2]), jnp.float32),
            pltpu.VMEM(shape, jnp.bfloat16),
            pltpu.SemaphoreType.DMA((CHUNKS,)),
            pltpu.SemaphoreType.DMA((2,)),
            pltpu.SemaphoreType.DMA((shape[0],)),
        ],
        compiler_params=pltpu.CompilerParams(vmem_limit_bytes=61 << 20),
        cost_estimate=pl.CostEstimate(
            flops=5_000_000_000, bytes_accessed=2 * tiles.size, transcendentals=0
        ),
    )(counts, rows, cols, tiles)


def flip(index, mask, n):
    out, bit = 0, 1
    while bit < n:
        have = (index // bit) % 2
        out = out + bit * ((1 - have) if mask & bit else have)
        bit *= 2
    return out


def combine_kernel(
    n_row, n_col, own_ref, x_ref, y_ref, across_ref, weight_ref, dense_hbm, out_ref,
    dense_ref, dense_sem, table, send, recv, gather_send, gather_recv, send_sems, recv_sems,
):
    me_row, me = lax.axis_index("row"), lax.axis_index("col")
    block = out_ref.shape[0]
    barrier = pltpu.get_barrier_semaphore()
    buddy = flip(me_row, 1, n_row)
    pl.semaphore_signal(barrier, inc=1, device_id=(buddy, me), device_id_type=MESH)
    for j in range(1, n_col):
        pl.semaphore_signal(
            barrier, inc=1, device_id=(me_row, (me + j) % n_col), device_id_type=MESH
        )
    dense_copy = pltpu.make_async_copy(dense_hbm, dense_ref, dense_sem.at[0])
    dense_copy.start()

    def rows_of(source):
        return pl.ds(pl.multiple_of(source * block, block), block)

    weight = weight_ref[...]
    sources = [flip(me_row, m, n_row) for m in (0, 2, 4, 6)]
    for source, ref in zip(sources, (own_ref, x_ref, y_ref, across_ref)):
        product = jnp.dot(ref[...], weight, preferred_element_type=jnp.float32)
        table[rows_of(source)] = product.astype(table.dtype)
    pl.semaphore_wait(barrier, n_col)

    pieces = []
    for k, source in enumerate(sources):
        part = table.at[rows_of(source)]
        copy = pltpu.make_async_remote_copy(
            src_ref=part,
            dst_ref=part,
            send_sem=gather_send.at[k],
            recv_sem=gather_recv.at[k],
            device_id=(buddy, me),
            device_id_type=MESH,
        )
        copy.start()
        pieces.append(copy)
    dense_copy.wait()
    for copy in pieces:
        copy.wait_recv()

    def partial(owner):
        at = rows_of(owner)
        left = jnp.concatenate([dense_ref[i, at] for i in range(dense_ref.shape[0])], axis=1)
        return jnp.dot(left, table[...], preferred_element_type=jnp.float32)

    copies = []
    for j in (2, 1, 3):
        peer = (me + j) % n_col
        send[j - 1] = partial(peer).astype(send.dtype)
        copy = pltpu.make_async_remote_copy(
            src_ref=send.at[j - 1],
            dst_ref=recv.at[j - 1],
            send_sem=send_sems.at[j - 1],
            recv_sem=recv_sems.at[j - 1],
            device_id=(me_row, peer),
            device_id_type=MESH,
        )
        copy.start()
        copies.append((j, copy))
    total = partial(me)
    for j, copy in copies:
        copy.wait_recv()
        total = total + recv[j - 1].astype(jnp.float32)
    out_ref[...] = jnp.maximum(total, 0.0).astype(out_ref.dtype)
    for copy in pieces:
        copy.wait_send()
    for j, copy in copies:
        copy.wait_send()


def fast_body(n_row, n_col, features, weight, tiles, tile_rows, tile_cols, counts):
    block, width = features.shape
    pieces = [features]
    for m in (2, 4, 6):
        pieces.append(lax.ppermute(features, "row", [(i, i ^ m) for i in range(n_row)]))
    dense = densify(
        counts, tile_rows, tile_cols, tiles, n_col * block // TILE, n_row * block // TILE
    )
    vmem = pl.BlockSpec(memory_space=pltpu.VMEM)
    return pl.pallas_call(
        functools.partial(combine_kernel, n_row, n_col),
        out_shape=jax.ShapeDtypeStruct((block, width), jnp.bfloat16),
        in_specs=[vmem] * 5 + [pl.BlockSpec(memory_space=pltpu.HBM)],
        out_specs=vmem,
        scratch_shapes=[
            pltpu.VMEM(dense.shape, dense.dtype),
            pltpu.SemaphoreType.DMA((1,)),
            pltpu.VMEM((n_row * block, width), jnp.bfloat16),
            pltpu.VMEM((n_col - 1, block, width), jnp.bfloat16),
            pltpu.VMEM((n_col - 1, block, width), jnp.bfloat16),
            pltpu.SemaphoreType.DMA((4,)),
            pltpu.SemaphoreType.DMA((4,)),
            pltpu.SemaphoreType.DMA((n_col - 1,)),
            pltpu.SemaphoreType.DMA((n_col - 1,)),
        ],
        compiler_params=pltpu.CompilerParams(
            collective_id=0, has_side_effects=True, vmem_limit_bytes=52 << 20
        ),
    )(*pieces, weight, dense)


def general_body(features, weight, tiles, tile_rows, tile_cols, counts):
    feature_width = weight.shape[1]
    product_rows = jnp.dot(features, weight, preferred_element_type=jnp.float32).astype(
        jnp.bfloat16
    )
    gathered = lax.all_gather(product_rows, "row", axis=0, tiled=True)
    column_table = gathered.reshape(gathered.shape[0] // TILE, TILE, feature_width)
    row_tiles = lax.axis_size("col") * features.shape[0] // TILE
    slot_count = tile_rows.shape[2]
    block_size = min(64, slot_count)
    half_block = block_size // 2
    passes = slot_count // block_size
    pair_list = tiles[0, 0]
    row_list = tile_rows[0, 0]
    col_list = tile_cols[0, 0]
    live_count = counts[0, 0]
    block_slots = jnp.arange(block_size, dtype=jnp.int32)

    def add_block(block_index, total):
        first = block_index * block_size
        pair_block = lax.dynamic_slice_in_dim(pair_list, block_index * half_block, half_block, 0)
        pair_block = pair_block.reshape(half_block, TILE, 2, TILE)
        row_block = lax.dynamic_slice_in_dim(row_list, first, block_size, 0)
        col_block = lax.dynamic_slice_in_dim(col_list, first, block_size, 0)
        picked = column_table[col_block].reshape(half_block, 2, TILE, feature_width)
        terms = jnp.einsum(
            "qajb,qjbf->qjaf", pair_block, picked, preferred_element_type=jnp.float32
        )
        terms = terms.reshape(block_size, TILE, feature_width)
        in_use = (first + block_slots < live_count).astype(jnp.float32)
        terms = terms * in_use[:, None, None]
        return total.at[row_block].add(terms)

    zero_total = jnp.zeros((row_tiles, TILE, feature_width), jnp.float32)
    total = lax.fori_loop(0, passes, add_block, zero_total)
    partial_value = total.reshape(row_tiles * TILE, feature_width)
    own_rows = lax.psum_scatter(partial_value, "col", scatter_dimension=0, tiled=True)
    return jnp.maximum(own_rows, 0.0).astype(jnp.bfloat16)


def solution(mesh):
    n_row, n_col = mesh.shape["row"], mesh.shape["col"]
    fast = (n_row, n_col) == (8, 4)
    body = functools.partial(fast_body, n_row, n_col) if fast else general_body
    return jax.shard_map(
        body,
        mesh=mesh,
        in_specs=(
            P(("row", "col"), None),
            P(),
            P("row", "col", None, None, None),
            P("row", "col", None),
            P("row", "col", None),
            P("row", "col"),
        ),
        out_specs=P(("row", "col"), None),
        check_vma=False,
    )
```
